32 devices in a mesh: expert: 8 (over y, x, core), tensor: 4 (over z).
Axes of the slice: x: 2, y: 2, z: 4, core: 2. Of those that a mesh axis runs over, the one named last changes fastest.
Arguments:
- tokens: bfloat16 [256, 2560], P(('expert', 'tensor')), may hold values from -12 to 12
- expert_ids: int32 [256], P(('expert', 'tensor')), may hold values from 0 to 7, as said below
- slot_ids: int32 [256], P(('expert', 'tensor')), may hold values from 0 to 7
- router: bfloat16 [2560, 8], replicated, may hold values from -0.125 to 0.125
- w_gate: bfloat16 [8, 2560, 4096], P('expert', None, 'tensor'), may hold values from -0.125 to 0.125
- w_up: bfloat16 [8, 2560, 4096], P('expert', None, 'tensor'), may hold values from -0.125 to 0.125
- hidden_grad: bfloat16 [8, 64, 4096], P('expert', None, 'tensor'), may hold values from -6 to 6
Outputs:
- activation: bfloat16 [8, 64, 4096], P('expert', None, 'tensor')
- token_grad: bfloat16 [256, 2560], P(('expert', 'tensor'))
The draws below stay inside these ranges and needn't reach their ends.
Inputs may be any that keep to these rules, and one draw needn't show every extreme that they name: expert_ids and slot_ids are drawn together. Within each aligned group of 32 consecutive tokens no two tokens share both expert and slot, so a group sends at most 8 tokens to one expert; in every draw one expert takes all 8 slots of every group.
All inputs are finite; a program needn't handle non-finite values.
Results may differ from the reference program's by a relative error of at most 0.02.
Values may be sent and summed in bfloat16 or wider, within the bound.
A program may use at most 64 MiB of HBM per device.

```python
import jax
import jax.numpy as jnp
from jax import lax

D = 2560
HID = 4096
EXPERTS = 8
TOKENS = 256
GROUP = 32
CAP = 8
ROWS = 64
N_TENSOR = 4


def routing_pair(key):
    base_key = jax.random.fold_in(key, 17)
    full_expert = jax.random.randint(jax.random.fold_in(base_key, 1), (), 0, EXPERTS)

    def one_group(group_key):
        rank_table = jax.random.permutation(group_key, EXPERTS * CAP).astype(jnp.int32)
        slot_grid = jnp.arange(EXPERTS * CAP, dtype=jnp.int32)
        extra_expert = jax.random.randint(jax.random.fold_in(group_key, 3), (), 0, EXPERTS)
        favoured = (slot_grid // CAP == full_expert) | (slot_grid // CAP == extra_expert)
        priority = jnp.where(favoured, rank_table - EXPERTS * CAP, rank_table)
        ordering = jnp.argsort(priority, stable=True)
        chosen_ids = ordering[:GROUP]
        shuffle = jax.random.permutation(jax.random.fold_in(group_key, 5), GROUP)
        chosen_ids = chosen_ids[shuffle].astype(jnp.int32)
        return (chosen_ids // CAP, chosen_ids % CAP)
    group_keys = jax.random.split(jax.random.fold_in(base_key, 2), TOKENS // GROUP)
    expert_table, slot_table = jax.vmap(one_group)(group_keys)
    return (expert_table.reshape(TOKENS).astype(jnp.int32), slot_table.reshape(TOKENS).astype(jnp.int32))


def draw_expert_ids(key, part):
    return routing_pair(key)[0]


def draw_slot_ids(key, part):
    return routing_pair(key)[1]


def levels(own_key, shape, cuts, low, high):
    gain, own = 1.0, jax.random.fold_in(own_key, 6)
    for dim, blocks in cuts:
        heights = jnp.exp(jax.random.uniform(jax.random.fold_in(own, dim), (blocks,), jnp.float32, low / len(cuts), high / len(cuts)))
        gain = gain * jnp.repeat(heights, shape[dim] // blocks).reshape([-1 if axis == dim else 1 for axis in range(len(shape))])
    return gain


def gaussian(own_key, extent, deviation, most, cuts=(), kind=jnp.bfloat16):
    entries = deviation * jax.random.normal(own_key, extent, jnp.float32)
    if cuts:
        entries = entries * levels(own_key, extent, cuts, -0.22, 0.18)
    return jnp.clip(entries, -most, most).astype(kind)


def setup_inputs(seed: int = 0) -> dict:
    keys = jax.random.split(jax.random.key(seed), 8)
    return {
        "tokens": gaussian(keys[0], (TOKENS, D), 2.0, 12.0, ((0, 32),)),
        "expert_ids": draw_expert_ids(jax.random.fold_in(keys[7], 71), 0),
        "slot_ids": draw_slot_ids(jax.random.fold_in(keys[7], 71), 0),
        "router": gaussian(keys[3], (D, EXPERTS), D ** -0.5, 0.125),
        "w_gate": gaussian(keys[4], (EXPERTS, D, HID), D ** -0.5, 0.125, ((0, 8), (2, 4))),
        "w_up": gaussian(keys[5], (EXPERTS, D, HID), D ** -0.5, 0.125, ((0, 8), (2, 4))),
        "hidden_grad": gaussian(keys[6], (EXPERTS, ROWS, HID), 1.0, 6.0, ((0, 8), (2, 4))),
    }


def silu_parts(gate_proj):
    sigma_gate = jax.nn.sigmoid(gate_proj)
    return gate_proj * sigma_gate, sigma_gate * (1.0 + gate_proj * (1.0 - sigma_gate))


def reference(tokens, expert_ids, slot_ids, router, w_gate, w_up, hidden_grad):
    logits = jnp.dot(tokens, router, preferred_element_type=jnp.float32)
    picked = jnp.take_along_axis(logits, expert_ids[:, None], axis=1)[:, 0]
    router_score = jax.nn.sigmoid(picked)
    routed_in = (router_score[:, None] * tokens.astype(jnp.float32)).astype(jnp.bfloat16)
    group_index = (jnp.arange(TOKENS, dtype=jnp.int32) // GROUP).astype(jnp.int32)
    target_row = (expert_ids * ROWS + group_index * CAP + slot_ids).astype(jnp.int32)
    dispatched = jnp.zeros((EXPERTS * ROWS, D), jnp.bfloat16).at[target_row].set(routed_in)
    dispatched = dispatched.reshape(EXPERTS, ROWS, D)
    hidden_piece = HID // N_TENSOR

    def per_expert(expert_item):
        routed_rows, gate_weight, up_weight, cotangent = expert_item
        gate_proj = jnp.dot(routed_rows, gate_weight, preferred_element_type=jnp.float32)
        lifted = jnp.dot(routed_rows, up_weight, preferred_element_type=jnp.float32)
        silu_gate, silu_slope = silu_parts(gate_proj)
        activation = (silu_gate * lifted).astype(jnp.bfloat16)
        cot_float = cotangent.astype(jnp.float32)
        d_gate = (cot_float * lifted * silu_slope).astype(jnp.bfloat16)
        d_lifted = (cot_float * silu_gate).astype(jnp.bfloat16)
        gate_blocks = d_gate.astype(jnp.float32).reshape(ROWS, N_TENSOR, hidden_piece)
        lift_blocks = d_lifted.astype(jnp.float32).reshape(ROWS, N_TENSOR, hidden_piece)
        gate_table = gate_weight.astype(jnp.float32).reshape(D, N_TENSOR, hidden_piece)
        up_table = up_weight.astype(jnp.float32).reshape(D, N_TENSOR, hidden_piece)
        partial_value = jnp.einsum('rtk,dtk->trd', gate_blocks, gate_table) + jnp.einsum('rtk,dtk->trd', lift_blocks, up_table)
        partial_value = lax.optimization_barrier(partial_value.astype(jnp.bfloat16)).astype(jnp.float32)
        d_rows = jnp.sum(partial_value, axis=0).astype(jnp.bfloat16)
        return activation, d_rows

    activation, d_dispatched = lax.map(per_expert, (dispatched, w_gate, w_up, hidden_grad))
    d_routed = d_dispatched.reshape(EXPERTS * ROWS, D)[target_row]
    d_float = d_routed.astype(jnp.float32)
    inner = jnp.sum(tokens.astype(jnp.float32) * d_float, axis=1)
    router_column = router.astype(jnp.float32).T[expert_ids]
    gradient = router_score[:, None] * d_float + (inner * router_score * (1.0 - router_score))[:, None] * router_column
    return activation, gradient.astype(jnp.bfloat16)
```

```python
import functools

import jax
import jax.numpy as jnp
from jax import lax
from jax.experimental import pallas as pl
from jax.experimental.pallas import tpu as pltpu
from jax.sharding import PartitionSpec as P

MESH = pl.DeviceIdType.MESH
F32 = jnp.float32
BF16 = jnp.bfloat16
LAG = 2


def each(count, body):
    if count <= 16:
        for index in range(count):
            body(index)
    else:

        def step(index, carry):
            body(index)
            return carry

        lax.fori_loop(0, count, step, 0)


def kernel(
    chunks,
    n_expert,
    n_tensor,
    tokens_hbm,
    expert_hbm,
    slot_hbm,
    router_hbm,
    gate_hbm,
    up_hbm,
    grad_hbm,
    act_hbm,
    out_hbm,
    tokens,
    expert_ids,
    slot_ids,
    router,
    w_gate,
    w_up,
    hidden_grad,
    act,
    out,
    ids,
    rows,
    sent,
    arrived,
    part,
    returned,
    mine,
    partials,
    acc_gate,
    acc_up,
    d_gate,
    d_lifted,
    d_rows,
    in_sem,
    w_sem,
    out_sem,
    ids_sem,
    rows_sem,
    slots_sem,
    part_sem,
    mine_sem,
):
    me_e = lax.axis_index("expert")
    me_t = lax.axis_index("tensor")
    tok_rows, width = tokens.shape
    piece = width // chunks
    capacity = arrived.shape[2]
    slots = n_expert * capacity
    group = n_tensor * tok_rows

    def span(c):
        return pl.ds(c * piece, piece)

    def peer_t(k):
        return lax.rem(me_t + k + 1, n_tensor)

    def peer_e(k):
        return lax.rem(me_e + k + 1, n_expert)

    def over_t(src, dst, sems, index, peer):
        return pltpu.make_async_remote_copy(
            src_ref=src,
            dst_ref=dst,
            send_sem=sems.at[(0, *index, peer)],
            recv_sem=sems.at[(1, *index, me_t)],
            device_id={"tensor": peer},
            device_id_type=MESH,
        )

    def over_e(src, dst, sems, index, peer):
        return pltpu.make_async_remote_copy(
            src_ref=src,
            dst_ref=dst,
            send_sem=sems.at[(0, *index, peer)],
            recv_sem=sems.at[(1, *index, me_e)],
            device_id={"expert": peer},
            device_id_type=MESH,
        )

    def landed(buffer, sems, index, peer, axis):
        pltpu.make_async_remote_copy(
            src_ref=buffer,
            dst_ref=buffer,
            send_sem=sems.at[(0, *index, peer)],
            recv_sem=sems.at[(1, *index, peer)],
            device_id={axis: peer},
            device_id_type=MESH,
        ).wait_recv()

    loads = [
        pltpu.make_async_copy(expert_hbm, expert_ids, in_sem.at[0]),
        pltpu.make_async_copy(slot_hbm, slot_ids, in_sem.at[1]),
        pltpu.make_async_copy(tokens_hbm, tokens, in_sem.at[2]),
        pltpu.make_async_copy(router_hbm, router, in_sem.at[3]),
        pltpu.make_async_copy(grad_hbm.at[0], hidden_grad, in_sem.at[4]),
    ]
    for load in loads[:4]:
        load.start()

    barrier = pltpu.get_barrier_semaphore()

    def greet_t(k):
        pl.semaphore_signal(
            barrier, inc=1, device_id={"tensor": peer_t(k)}, device_id_type=MESH
        )

    def greet_e(k):
        pl.semaphore_signal(
            barrier, inc=1, device_id={"expert": peer_e(k)}, device_id_type=MESH
        )

    each(n_tensor - 1, greet_t)
    each(n_expert - 1, greet_e)

    weight_loads = []
    for c in range(chunks):
        pair = (
            pltpu.make_async_copy(gate_hbm.at[0, span(c)], w_gate.at[span(c)], w_sem.at[0, c]),
            pltpu.make_async_copy(up_hbm.at[0, span(c)], w_up.at[span(c)], w_sem.at[1, c]),
        )
        weight_loads.append(pair)
        for load in pair:
            load.start()
    loads[4].start()

    loads[0].wait()
    loads[1].wait()
    row_index = lax.broadcasted_iota(jnp.int32, (tok_rows, 128), 0)
    expert_of = jnp.zeros((tok_rows, 128), jnp.int32)
    slot_of = jnp.zeros((tok_rows, 128), jnp.int32)
    for i in range(tok_rows):
        expert_of = jnp.where(row_index == i, expert_ids[i], expert_of)
        slot_of = jnp.where(row_index == i, slot_ids[i], slot_of)
    ids[me_t] = expert_of * capacity + slot_of
    picked = (
        expert_of[:, :1] == lax.broadcasted_iota(jnp.int32, (tok_rows, n_expert), 1)
    ).astype(F32)

    loads[2].wait()
    loads[3].wait()
    column = jnp.dot(picked.astype(BF16), router[...], preferred_element_type=F32)
    token_values = tokens[...].astype(F32)
    score = jax.nn.sigmoid(jnp.sum(token_values * column, axis=1, keepdims=True))
    routed = (score * token_values).astype(BF16)
    for c in range(chunks):
        rows[c, me_t] = routed[:, c * piece : (c + 1) * piece]

    pl.semaphore_wait(barrier, n_tensor + n_expert - 2)

    def send_ids(k):
        over_t(ids.at[me_t], ids.at[me_t], ids_sem, (), peer_t(k)).start()

    each(n_tensor - 1, send_ids)
    for c in range(chunks):

        def send_rows(k):
            over_t(rows.at[c, me_t], rows.at[c, me_t], rows_sem, (c,), peer_t(k)).start()

        each(n_tensor - 1, send_rows)

    each(n_tensor - 1, lambda k: landed(ids.at[peer_t(k)], ids_sem, (), peer_t(k), "tensor"))
    target = ids[...].reshape(group, 128)[:, :1]
    place = (target == lax.broadcasted_iota(jnp.int32, (group, slots), 1)).astype(F32).astype(BF16)

    def dispatch(c):
        each(
            n_tensor - 1,
            lambda k: landed(rows.at[c, peer_t(k)], rows_sem, (c,), peer_t(k), "tensor"),
        )
        group_rows = rows[c].astype(F32).reshape(group, piece).astype(BF16)
        placed = lax.dot_general(
            place, group_rows, (((0,), (0,)), ((), ())), preferred_element_type=F32
        )
        sent[c] = placed.reshape(n_expert, capacity, piece).astype(BF16)

        def send(k):
            peer = peer_e(k)
            over_e(sent.at[c, peer], arrived.at[c, me_e], slots_sem, (c,), peer).start()

        each(n_expert - 1, send)
        arrived[c, me_e] = sent[c, me_e]

    def project(c):
        each(
            n_expert - 1,
            lambda k: landed(arrived.at[c, peer_e(k)], slots_sem, (c,), peer_e(k), "expert"),
        )
        for load in weight_loads[c]:
            load.wait()
        lhs = arrived[c].astype(F32).reshape(slots, piece).astype(BF16)
        for total, weight in ((acc_gate, w_gate), (acc_up, w_up)):
            product = jnp.dot(lhs, weight[span(c)], preferred_element_type=F32)
            total[...] = product if c == 0 else total[...] + product

    for step in range(chunks + LAG):
        if step < chunks:
            dispatch(step)
        if step >= LAG:
            project(step - LAG)

    loads[4].wait()
    gate_proj = acc_gate[...]
    lifted = acc_up[...]
    cotangent = hidden_grad[...].astype(F32)
    sigma = jax.nn.sigmoid(gate_proj)
    silu = gate_proj * sigma
    slope = sigma * (1.0 + gate_proj * (1.0 - sigma))
    d_gate[...] = (cotangent * lifted * slope).astype(BF16)
    d_lifted[...] = (cotangent * silu).astype(BF16)
    act[...] = (silu * lifted).astype(BF16)
    store_act = pltpu.make_async_copy(act, act_hbm.at[0], out_sem.at[0])
    store_act.start()

    contract = (((1,), (1,)), ((), ()))

    def pull_back(c):
        value = lax.dot_general(
            d_gate[...], w_gate[span(c)], contract, preferred_element_type=F32
        ) + lax.dot_general(d_lifted[...], w_up[span(c)], contract, preferred_element_type=F32)
        part[c] = value.reshape(n_expert, capacity, piece).astype(BF16)

        def send(k):
            peer = peer_e(k)
            over_e(part.at[c, peer], returned.at[c, me_e], part_sem, (c,), peer).start()

        each(n_expert - 1, send)
        returned[c, me_e] = part[c, me_e]

    def collect(c):
        each(
            n_expert - 1,
            lambda k: landed(returned.at[c, peer_e(k)], part_sem, (c,), peer_e(k), "expert"),
        )
        slot_rows = returned[c].astype(F32).reshape(slots, piece).astype(BF16)
        token_rows = jnp.dot(place, slot_rows, preferred_element_type=F32)
        mine[c] = token_rows.reshape(n_tensor, tok_rows, piece).astype(BF16)

        def send(k):
            peer = peer_t(k)
            over_t(mine.at[c, peer], partials.at[c, me_t], mine_sem, (c,), peer).start()

        each(n_tensor - 1, send)
        partials[c, me_t] = mine[c, me_t]

    def add_up(c):
        each(
            n_tensor - 1,
            lambda k: landed(partials.at[c, peer_t(k)], mine_sem, (c,), peer_t(k), "tensor"),
        )
        summed = jnp.sum(partials[c].astype(F32), axis=0).astype(BF16).astype(F32)
        d_rows[:, span(c)] = summed
        return jnp.sum(
            token_values[:, c * piece : (c + 1) * piece] * summed, axis=1, keepdims=True
        )

    inner = jnp.zeros((tok_rows, 1), F32)
    for step in range(chunks + 2 * LAG):
        if step < chunks:
            pull_back(step)
        if LAG <= step < chunks + LAG:
            collect(step - LAG)
        if step >= 2 * LAG:
            inner = inner + add_up(step - 2 * LAG)

    gradient = score * d_rows[...] + (inner * score * (1.0 - score)) * column
    out[...] = gradient.astype(BF16)
    store_out = pltpu.make_async_copy(out, out_hbm, out_sem.at[1])
    store_out.start()

    def ids_gone(k):
        over_t(ids.at[me_t], ids.at[me_t], ids_sem, (), peer_t(k)).wait_send()

    each(n_tensor - 1, ids_gone)
    for c in range(chunks):

        def gone_t(k):
            peer = peer_t(k)
            over_t(rows.at[c, me_t], rows.at[c, me_t], rows_sem, (c,), peer).wait_send()
            over_t(mine.at[c, peer], partials.at[c, me_t], mine_sem, (c,), peer).wait_send()

        def gone_e(k):
            peer = peer_e(k)
            over_e(sent.at[c, peer], arrived.at[c, me_e], slots_sem, (c,), peer).wait_send()
            over_e(part.at[c, peer], returned.at[c, me_e], part_sem, (c,), peer).wait_send()

        each(n_tensor - 1, gone_t)
        each(n_expert - 1, gone_e)
    store_act.wait()
    store_out.wait()


def shards(tokens, expert_ids, slot_ids, router, w_gate, w_up, hidden_grad):
    n_tensor = lax.axis_size("tensor")
    n_expert = lax.axis_size("expert")
    tok_rows, width = tokens.shape
    slots, hidden = hidden_grad.shape[1:]
    capacity = slots // n_expert
    piece = max(p for p in range(128, 513, 128) if width % p == 0)
    chunks = width // piece
    by_expert = (chunks, n_expert, capacity, piece)
    by_tensor = (chunks, n_tensor, tok_rows, piece)
    dma = pltpu.SemaphoreType.DMA
    hbm = pl.BlockSpec(memory_space=pltpu.HBM)
    return pl.pallas_call(
        functools.partial(kernel, chunks, n_expert, n_tensor),
        out_shape=(
            jax.ShapeDtypeStruct(hidden_grad.shape, BF16),
            jax.ShapeDtypeStruct(tokens.shape, BF16),
        ),
        in_specs=[hbm] * 7,
        out_specs=(hbm, hbm),
        scratch_shapes=[
            pltpu.VMEM(tokens.shape, BF16),
            pltpu.SMEM(expert_ids.shape, jnp.int32),
            pltpu.SMEM(slot_ids.shape, jnp.int32),
            pltpu.VMEM(router.shape[::-1], BF16),
            pltpu.VMEM(w_gate.shape[1:], BF16),
            pltpu.VMEM(w_up.shape[1:], BF16),
            pltpu.VMEM((slots, hidden), BF16),
            pltpu.VMEM((slots, hidden), BF16),
            pltpu.VMEM(tokens.shape, BF16),
            pltpu.VMEM((n_tensor, tok_rows, 128), jnp.int32),
            pltpu.VMEM(by_tensor, BF16),
            pltpu.VMEM(by_expert, BF16),
            pltpu.VMEM(by_expert, BF16),
            pltpu.VMEM(by_expert, BF16),
            pltpu.VMEM(by_expert, BF16),
            pltpu.VMEM(by_tensor, BF16),
            pltpu.VMEM(by_tensor, BF16),
            pltpu.VMEM((slots, hidden), F32),
            pltpu.VMEM((slots, hidden), F32),
            pltpu.VMEM((slots, hidden), BF16),
            pltpu.VMEM((slots, hidden), BF16),
            pltpu.VMEM(tokens.shape, F32),
            dma((5,)),
            dma((2, chunks)),
            dma((2,)),
            dma((2, n_tensor)),
            dma((2, chunks, n_tensor)),
            dma((2, chunks, n_expert)),
            dma((2, chunks, n_expert)),
            dma((2, chunks, n_tensor)),
        ],
        compiler_params=pltpu.CompilerParams(
            collective_id=0, has_side_effects=True, vmem_limit_bytes=56 * 1024 * 1024
        ),
        name="routed_experts",
    )(tokens, expert_ids, slot_ids, router.T, w_gate, w_up, hidden_grad)


def solution(mesh):
    in_specs = (
        P(("expert", "tensor"), None),
        P(("expert", "tensor")),
        P(("expert", "tensor")),
        P(),
        P("expert", None, "tensor"),
        P("expert", None, "tensor"),
        P("expert", None, "tensor"),
    )
    out_specs = (P("expert", None, "tensor"), P(("expert", "tensor"), None))
    return jax.shard_map(shards, mesh=mesh, in_specs=in_specs, out_specs=out_specs, check_vma=False)
```

```python
import functools

import jax
import jax.numpy as jnp
from jax import lax
from jax.experimental import pallas as pl
from jax.experimental.pallas import tpu as pltpu
from jax.sharding import PartitionSpec as P

MESH = pl.DeviceIdType.MESH
F32 = jnp.float32
BF16 = jnp.bfloat16
LAG = 2


def each(count, body):
    if count <= 16:
        for index in range(count):
            body(index)
    else:

        def step(index, carry):
            body(index)
            return carry

        lax.fori_loop(0, count, step, 0)


def kernel(
    chunks,
    n_expert,
    n_tensor,
    tokens_hbm,
    expert_hbm,
    slot_hbm,
    router_hbm,
    gate_hbm,
    up_hbm,
    grad_hbm,
    act,
    out,
    tokens,
    expert_ids,
    slot_ids,
    router,
    w_gate,
    w_up,
    hidden_grad,
    ids,
    rows,
    sent,
    arrived,
    part,
    returned,
    mine,
    partials,
    acc_gate,
    acc_up,
    d_gate,
    d_lifted,
    d_rows,
    in_sem,
    w_sem,
    ids_sem,
    rows_sem,
    slots_sem,
    part_sem,
    mine_sem,
):
    me_e = lax.axis_index("expert")
    me_t = lax.axis_index("tensor")
    tok_rows, width = tokens.shape
    piece = width // chunks
    capacity = arrived.shape[2]
    slots = n_expert * capacity
    group = n_tensor * tok_rows

    def span(c):
        return pl.ds(c * piece, piece)

    def peer_t(k):
        return lax.rem(me_t + k + 1, n_tensor)

    def peer_e(k):
        return lax.rem(me_e + k + 1, n_expert)

    def over_t(src, dst, sems, index, peer):
        return pltpu.make_async_remote_copy(
            src_ref=src,
            dst_ref=dst,
            send_sem=sems.at[0, index],
            recv_sem=sems.at[1, index],
            device_id={"tensor": peer},
            device_id_type=MESH,
        )

    def over_e(src, dst, sems, index, peer):
        return pltpu.make_async_remote_copy(
            src_ref=src,
            dst_ref=dst,
            send_sem=sems.at[0, index],
            recv_sem=sems.at[1, index],
            device_id={"expert": peer},
            device_id_type=MESH,
        )

    def landed(buffer, sems, index, count):
        whole = buffer.at[pl.ds(0, count)]
        pltpu.make_async_copy(whole, whole, sems.at[1, index]).wait()

    def left(buffer, sems, index, count):
        whole = buffer.at[pl.ds(0, count)]
        pltpu.make_async_copy(whole, whole, sems.at[0, index]).wait()

    loads = [
        pltpu.make_async_copy(expert_hbm, expert_ids, in_sem.at[0]),
        pltpu.make_async_copy(slot_hbm, slot_ids, in_sem.at[1]),
        pltpu.make_async_copy(tokens_hbm, tokens, in_sem.at[2]),
        pltpu.make_async_copy(router_hbm, router, in_sem.at[3]),
        pltpu.make_async_copy(grad_hbm.at[0], hidden_grad, in_sem.at[4]),
    ]
    for load in loads[:4]:
        load.start()

    barrier = pltpu.get_barrier_semaphore()

    def greet_t(k):
        pl.semaphore_signal(
            barrier, inc=1, device_id={"tensor": peer_t(k)}, device_id_type=MESH
        )

    def greet_e(k):
        pl.semaphore_signal(
            barrier, inc=1, device_id={"expert": peer_e(k)}, device_id_type=MESH
        )

    each(n_tensor - 1, greet_t)
    each(n_expert - 1, greet_e)

    weight_loads = []
    for c in range(chunks):
        pair = (
            pltpu.make_async_copy(gate_hbm.at[0, span(c)], w_gate.at[span(c)], w_sem.at[0, c]),
            pltpu.make_async_copy(up_hbm.at[0, span(c)], w_up.at[span(c)], w_sem.at[1, c]),
        )
        weight_loads.append(pair)
        for load in pair:
            load.start()
    loads[4].start()

    loads[0].wait()
    loads[1].wait()
    row_index = lax.broadcasted_iota(jnp.int32, (tok_rows, 128), 0)
    expert_of = jnp.zeros((tok_rows, 128), jnp.int32)
    slot_of = jnp.zeros((tok_rows, 128), jnp.int32)
    for i in range(tok_rows):
        expert_of = jnp.where(row_index == i, expert_ids[i], expert_of)
        slot_of = jnp.where(row_index == i, slot_ids[i], slot_of)
    ids[me_t] = expert_of * capacity + slot_of
    picked = (
        expert_of[:, :1] == lax.broadcasted_iota(jnp.int32, (tok_rows, n_expert), 1)
    ).astype(F32)

    loads[2].wait()
    loads[3].wait()
    column = jnp.dot(picked.astype(BF16), router[...], preferred_element_type=F32)
    token_values = tokens[...].astype(F32)
    score = jax.nn.sigmoid(jnp.sum(token_values * column, axis=1, keepdims=True))
    routed = (score * token_values).astype(BF16)
    for c in range(chunks):
        rows[c, me_t] = routed[:, c * piece : (c + 1) * piece]

    pl.semaphore_wait(barrier, n_tensor + n_expert - 2)

    def send_ids(k):
        over_t(ids.at[me_t], ids.at[me_t], ids_sem, 0, peer_t(k)).start()

    each(n_tensor - 1, send_ids)
    for c in range(chunks):

        def send_rows(k):
            over_t(rows.at[c, me_t], rows.at[c, me_t], rows_sem, c, peer_t(k)).start()

        each(n_tensor - 1, send_rows)

    landed(ids, ids_sem, 0, n_tensor - 1)
    target = ids[...].reshape(group, 128)[:, :1]
    place = (target == lax.broadcasted_iota(jnp.int32, (group, slots), 1)).astype(F32).astype(BF16)

    def dispatch(c):
        landed(rows.at[c], rows_sem, c, n_tensor - 1)
        group_rows = rows[c].astype(F32).reshape(group, piece).astype(BF16)
        placed = lax.dot_general(
            place, group_rows, (((0,), (0,)), ((), ())), preferred_element_type=F32
        )
        sent[c] = placed.reshape(n_expert, capacity, piece).astype(BF16)

        def send(k):
            peer = peer_e(k)
            over_e(sent.at[c, peer], arrived.at[c, me_e], slots_sem, c, peer).start()

        each(n_expert - 1, send)
        arrived[c, me_e] = sent[c, me_e]

    def project(c):
        landed(arrived.at[c], slots_sem, c, n_expert - 1)
        for load in weight_loads[c]:
            load.wait()
        lhs = arrived[c].astype(F32).reshape(slots, piece).astype(BF16)
        for total, weight in ((acc_gate, w_gate), (acc_up, w_up)):
            product = jnp.dot(lhs, weight[span(c)], preferred_element_type=F32)
            total[...] = product if c == 0 else total[...] + product

    for step in range(chunks + LAG):
        if step < chunks:
            dispatch(step)
        if step >= LAG:
            project(step - LAG)

    loads[4].wait()
    gate_proj = acc_gate[...]
    lifted = acc_up[...]
    cotangent = hidden_grad[...].astype(F32)
    sigma = jax.nn.sigmoid(gate_proj)
    silu = gate_proj * sigma
    slope = sigma * (1.0 + gate_proj * (1.0 - sigma))
    d_gate[...] = (cotangent * lifted * slope).astype(BF16)
    d_lifted[...] = (cotangent * silu).astype(BF16)
    act[0] = (silu * lifted).astype(BF16)

    contract = (((1,), (1,)), ((), ()))

    def pull_back(c):
        value = lax.dot_general(
            d_gate[...], w_gate[span(c)], contract, preferred_element_type=F32
        ) + lax.dot_general(d_lifted[...], w_up[span(c)], contract, preferred_element_type=F32)
        part[c] = value.reshape(n_expert, capacity, piece).astype(BF16)

        def send(k):
            peer = peer_e(k)
            over_e(part.at[c, peer], returned.at[c, me_e], part_sem, c, peer).start()

        each(n_expert - 1, send)
        returned[c, me_e] = part[c, me_e]

    def collect(c):
        landed(returned.at[c], part_sem, c, n_expert - 1)
        slot_rows = returned[c].astype(F32).reshape(slots, piece).astype(BF16)
        token_rows = jnp.dot(place, slot_rows, preferred_element_type=F32)
        mine[c] = token_rows.reshape(n_tensor, tok_rows, piece).astype(BF16)

        def send(k):
            peer = peer_t(k)
            over_t(mine.at[c, peer], partials.at[c, me_t], mine_sem, c, peer).start()

        each(n_tensor - 1, send)
        partials[c, me_t] = mine[c, me_t]

    def add_up(c):
        landed(partials.at[c], mine_sem, c, n_tensor - 1)
        summed = jnp.sum(partials[c].astype(F32), axis=0).astype(BF16).astype(F32)
        d_rows[:, span(c)] = summed
        return jnp.sum(
            token_values[:, c * piece : (c + 1) * piece] * summed, axis=1, keepdims=True
        )

    inner = jnp.zeros((tok_rows, 1), F32)
    for step in range(chunks + 2 * LAG):
        if step < chunks:
            pull_back(step)
        if LAG <= step < chunks + LAG:
            collect(step - LAG)
        if step >= 2 * LAG:
            inner = inner + add_up(step - 2 * LAG)

    gradient = score * d_rows[...] + (inner * score * (1.0 - score)) * column
    out[...] = gradient.astype(BF16)

    left(ids, ids_sem, 0, n_tensor - 1)
    for c in range(chunks):
        left(rows.at[c], rows_sem, c, n_tensor - 1)
        left(sent.at[c], slots_sem, c, n_expert - 1)
        left(part.at[c], part_sem, c, n_expert - 1)
        left(mine.at[c], mine_sem, c, n_tensor - 1)


def finish(act_in, out_in, act_out, out_out, sem):
    copies = (
        pltpu.make_async_copy(act_in, act_out, sem.at[0]),
        pltpu.make_async_copy(out_in, out_out, sem.at[1]),
    )
    for copy in copies:
        copy.start()
    for copy in copies:
        copy.wait()


def shards(tokens, expert_ids, slot_ids, router, w_gate, w_up, hidden_grad):
    n_tensor = lax.axis_size("tensor")
    n_expert = lax.axis_size("expert")
    tok_rows, width = tokens.shape
    slots, hidden = hidden_grad.shape[1:]
    capacity = slots // n_expert
    piece = max(p for p in range(128, 513, 128) if width % p == 0)
    chunks = width // piece
    by_expert = (chunks, n_expert, capacity, piece)
    by_tensor = (chunks, n_tensor, tok_rows, piece)
    dma = pltpu.SemaphoreType.DMA
    hbm = pl.BlockSpec(memory_space=pltpu.HBM)
    vmem = pl.BlockSpec(memory_space=pltpu.VMEM)
    out_shape = (
        jax.ShapeDtypeStruct(hidden_grad.shape, BF16),
        jax.ShapeDtypeStruct(tokens.shape, BF16),
    )
    results = pl.pallas_call(
        functools.partial(kernel, chunks, n_expert, n_tensor),
        out_shape=(pltpu.VMEM(hidden_grad.shape, BF16), pltpu.VMEM(tokens.shape, BF16)),
        in_specs=[hbm] * 7,
        out_specs=(vmem, vmem),
        scratch_shapes=[
            pltpu.VMEM(tokens.shape, BF16),
            pltpu.SMEM(expert_ids.shape, jnp.int32),
            pltpu.SMEM(slot_ids.shape, jnp.int32),
            pltpu.VMEM(router.shape[::-1], BF16),
            pltpu.VMEM(w_gate.shape[1:], BF16),
            pltpu.VMEM(w_up.shape[1:], BF16),
            pltpu.VMEM((slots, hidden), BF16),
            pltpu.VMEM((n_tensor, tok_rows, 128), jnp.int32),
            pltpu.VMEM(by_tensor, BF16),
            pltpu.VMEM(by_expert, BF16),
            pltpu.VMEM(by_expert, BF16),
            pltpu.VMEM(by_expert, BF16),
            pltpu.VMEM(by_expert, BF16),
            pltpu.VMEM(by_tensor, BF16),
            pltpu.VMEM(by_tensor, BF16),
            pltpu.VMEM((slots, hidden), F32),
            pltpu.VMEM((slots, hidden), F32),
            pltpu.VMEM((slots, hidden), BF16),
            pltpu.VMEM((slots, hidden), BF16),
            pltpu.VMEM(tokens.shape, F32),
            dma((5,)),
            dma((2, chunks)),
            dma((2, 1)),
            dma((2, chunks)),
            dma((2, chunks)),
            dma((2, chunks)),
            dma((2, chunks)),
        ],
        compiler_params=pltpu.CompilerParams(
            collective_id=0, has_side_effects=True, vmem_limit_bytes=56 * 1024 * 1024
        ),
        name="routed_experts",
    )(tokens, expert_ids, slot_ids, router.T, w_gate, w_up, hidden_grad)
    return pl.pallas_call(
        finish,
        out_shape=out_shape,
        in_specs=[vmem] * 2,
        out_specs=(hbm, hbm),
        scratch_shapes=[dma((2,))],
        name="move_results",
    )(*results)


def solution(mesh):
    in_specs = (
        P(("expert", "tensor"), None),
        P(("expert", "tensor")),
        P(("expert", "tensor")),
        P(),
        P("expert", None, "tensor"),
        P("expert", None, "tensor"),
        P("expert", None, "tensor"),
    )
    out_specs = (P("expert", None, "tensor"), P(("expert", "tensor"), None))
    return jax.shard_map(shards, mesh=mesh, in_specs=in_specs, out_specs=out_specs, check_vma=False)
```

```python
import functools

import jax
import jax.numpy as jnp
from jax import lax
from jax.experimental import pallas as pl
from jax.experimental.pallas import tpu as pltpu
from jax.sharding import PartitionSpec as P

MESH = pl.DeviceIdType.MESH
F32 = jnp.float32
BF16 = jnp.bfloat16
LAG = 1


def each(count, body):
    if count <= 16:
        for index in range(count):
            body(index)
    else:

        def step(index, carry):
            body(index)
            return carry

        lax.fori_loop(0, count, step, 0)


def kernel(
    chunks,
    n_expert,
    n_tensor,
    tokens_hbm,
    expert_hbm,
    slot_hbm,
    router_hbm,
    gate_hbm,
    up_hbm,
    grad_hbm,
    act,
    out,
    tokens,
    expert_ids,
    slot_ids,
    router,
    w_gate,
    w_up,
    hidden_grad,
    ids,
    rows,
    sent,
    arrived,
    part,
    returned,
    mine,
    partials,
    acc_gate,
    acc_up,
    d_gate,
    d_lifted,
    d_rows,
    in_sem,
    w_sem,
    ids_sem,
    rows_sem,
    slots_sem,
    part_sem,
    mine_sem,
):
    me_e = lax.axis_index("expert")
    me_t = lax.axis_index("tensor")
    tok_rows, width = tokens.shape
    piece = width // chunks
    capacity = arrived.shape[2]
    slots = n_expert * capacity
    group = n_tensor * tok_rows

    def span(c):
        return pl.ds(c * piece, piece)

    def peer_t(k):
        return lax.rem(me_t + k + 1, n_tensor)

    def peer_e(k):
        return lax.rem(me_e + k + 1, n_expert)

    def over_t(src, dst, sems, index, peer):
        return pltpu.make_async_remote_copy(
            src_ref=src,
            dst_ref=dst,
            send_sem=sems.at[0, index],
            recv_sem=sems.at[1, index],
            device_id={"tensor": peer},
            device_id_type=MESH,
        )

    def over_e(src, dst, sems, index, peer):
        return pltpu.make_async_remote_copy(
            src_ref=src,
            dst_ref=dst,
            send_sem=sems.at[0, index],
            recv_sem=sems.at[1, index],
            device_id={"expert": peer},
            device_id_type=MESH,
        )

    def landed(buffer, sems, index, count):
        whole = buffer.at[pl.ds(0, count)]
        pltpu.make_async_copy(whole, whole, sems.at[1, index]).wait()

    def left(buffer, sems, index, count):
        whole = buffer.at[pl.ds(0, count)]
        pltpu.make_async_copy(whole, whole, sems.at[0, index]).wait()

    loads = [
        pltpu.make_async_copy(expert_hbm, expert_ids, in_sem.at[0]),
        pltpu.make_async_copy(slot_hbm, slot_ids, in_sem.at[1]),
        pltpu.make_async_copy(tokens_hbm, tokens, in_sem.at[2]),
        pltpu.make_async_copy(router_hbm, router, in_sem.at[3]),
        pltpu.make_async_copy(grad_hbm.at[0], hidden_grad, in_sem.at[4]),
    ]
    for load in loads[:4]:
        load.start()

    barrier = pltpu.get_barrier_semaphore()

    def greet_t(k):
        pl.semaphore_signal(
            barrier, inc=1, device_id={"tensor": peer_t(k)}, device_id_type=MESH
        )

    def greet_e(k):
        pl.semaphore_signal(
            barrier, inc=1, device_id={"expert": peer_e(k)}, device_id_type=MESH
        )

    each(n_tensor - 1, greet_t)
    each(n_expert - 1, greet_e)

    weight_loads = []
    for c in range(chunks):
        pair = (
            pltpu.make_async_copy(gate_hbm.at[0, span(c)], w_gate.at[span(c)], w_sem.at[0, c]),
            pltpu.make_async_copy(up_hbm.at[0, span(c)], w_up.at[span(c)], w_sem.at[1, c]),
        )
        weight_loads.append(pair)
        for load in pair:
            load.start()
    loads[4].start()

    loads[0].wait()
    loads[1].wait()
    row_index = lax.broadcasted_iota(jnp.int32, (tok_rows, 128), 0)
    expert_of = jnp.zeros((tok_rows, 128), jnp.int32)
    slot_of = jnp.zeros((tok_rows, 128), jnp.int32)
    for i in range(tok_rows):
        expert_of = jnp.where(row_index == i, expert_ids[i], expert_of)
        slot_of = jnp.where(row_index == i, slot_ids[i], slot_of)
    ids[me_t] = expert_of * capacity + slot_of
    picked = (
        expert_of[:, :1] == lax.broadcasted_iota(jnp.int32, (tok_rows, n_expert), 1)
    ).astype(F32)

    loads[2].wait()
    loads[3].wait()
    column = jnp.dot(picked.astype(BF16), router[...], preferred_element_type=F32)
    token_values = tokens[...].astype(F32)
    score = jax.nn.sigmoid(jnp.sum(token_values * column, axis=1, keepdims=True))
    routed = (score * token_values).astype(BF16)
    for c in range(chunks):
        rows[c, me_t] = routed[:, c * piece : (c + 1) * piece]

    pl.semaphore_wait(barrier, n_tensor + n_expert - 2)

    def send_ids(k):
        over_t(ids.at[me_t], ids.at[me_t], ids_sem, 0, peer_t(k)).start()

    each(n_tensor - 1, send_ids)
    for c in range(chunks):

        def send_rows(k):
            over_t(rows.at[c, me_t], rows.at[c, me_t], rows_sem, c, peer_t(k)).start()

        each(n_tensor - 1, send_rows)

    landed(ids, ids_sem, 0, n_tensor - 1)
    target = ids[...].reshape(group, 128)[:, :1]
    place = (target == lax.broadcasted_iota(jnp.int32, (group, slots), 1)).astype(F32)
    place_t = place.T.astype(BF16)
    place = place.astype(BF16)

    def dispatch(c):
        landed(rows.at[c], rows_sem, c, n_tensor - 1)
        group_rows = rows[c].astype(F32).reshape(group, piece).astype(BF16)
        placed = jnp.dot(place_t, group_rows, preferred_element_type=F32)
        sent[c] = placed.reshape(n_expert, capacity, piece).astype(BF16)

        def send(k):
            peer = peer_e(k)
            over_e(sent.at[c, peer], arrived.at[c, me_e], slots_sem, c, peer).start()

        each(n_expert - 1, send)
        arrived[c, me_e] = sent[c, me_e]

    def project(c):
        landed(arrived.at[c], slots_sem, c, n_expert - 1)
        for load in weight_loads[c]:
            load.wait()
        lhs = arrived[c].astype(F32).reshape(slots, piece).astype(BF16)
        for total, weight in ((acc_gate, w_gate), (acc_up, w_up)):
            product = jnp.dot(lhs, weight[span(c)], preferred_element_type=F32)
            total[...] = product if c == 0 else total[...] + product

    for step in range(chunks + LAG):
        if step < chunks:
            dispatch(step)
        if step >= LAG:
            project(step - LAG)

    loads[4].wait()
    gate_proj = acc_gate[...]
    lifted = acc_up[...]
    cotangent = hidden_grad[...].astype(F32)
    sigma = jax.nn.sigmoid(gate_proj)
    silu = gate_proj * sigma
    slope = sigma * (1.0 + gate_proj * (1.0 - sigma))
    d_gate[...] = (cotangent * lifted * slope).astype(BF16)
    d_lifted[...] = (cotangent * silu).astype(BF16)
    act[0] = (silu * lifted).astype(BF16)

    contract = (((1,), (1,)), ((), ()))

    def pull_back(c):
        value = lax.dot_general(
            d_gate[...], w_gate[span(c)], contract, preferred_element_type=F32
        ) + lax.dot_general(d_lifted[...], w_up[span(c)], contract, preferred_element_type=F32)
        part[c] = value.reshape(n_expert, capacity, piece).astype(BF16)

        def send(k):
            peer = peer_e(k)
            over_e(part.at[c, peer], returned.at[c, me_e], part_sem, c, peer).start()

        each(n_expert - 1, send)
        returned[c, me_e] = part[c, me_e]

    def collect(c):
        landed(returned.at[c], part_sem, c, n_expert - 1)
        slot_rows = returned[c].astype(F32).reshape(slots, piece).astype(BF16)
        token_rows = jnp.dot(place, slot_rows, preferred_element_type=F32)
        mine[c] = token_rows.reshape(n_tensor, tok_rows, piece).astype(BF16)

        def send(k):
            peer = peer_t(k)
            over_t(mine.at[c, peer], partials.at[c, me_t], mine_sem, c, peer).start()

        each(n_tensor - 1, send)
        partials[c, me_t] = mine[c, me_t]

    def add_up(c):
        landed(partials.at[c], mine_sem, c, n_tensor - 1)
        summed = jnp.sum(partials[c].astype(F32), axis=0).astype(BF16).astype(F32)
        d_rows[:, span(c)] = summed
        return jnp.sum(
            token_values[:, c * piece : (c + 1) * piece] * summed, axis=1, keepdims=True
        )

    inner = jnp.zeros((tok_rows, 1), F32)
    for step in range(chunks + 2 * LAG):
        if step < chunks:
            pull_back(step)
        if LAG <= step < chunks + LAG:
            collect(step - LAG)
        if step >= 2 * LAG:
            inner = inner + add_up(step - 2 * LAG)

    gradient = score * d_rows[...] + (inner * score * (1.0 - score)) * column
    out[...] = gradient.astype(BF16)

    left(ids, ids_sem, 0, n_tensor - 1)
    for c in range(chunks):
        left(rows.at[c], rows_sem, c, n_tensor - 1)
        left(sent.at[c], slots_sem, c, n_expert - 1)
        left(part.at[c], part_sem, c, n_expert - 1)
        left(mine.at[c], mine_sem, c, n_tensor - 1)


def shards(tokens, expert_ids, slot_ids, router, w_gate, w_up, hidden_grad):
    n_tensor = lax.axis_size("tensor")
    n_expert = lax.axis_size("expert")
    tok_rows, width = tokens.shape
    slots, hidden = hidden_grad.shape[1:]
    capacity = slots // n_expert
    piece = max(p for p in range(128, 1281, 128) if width % p == 0)
    chunks = width // piece
    by_expert = (chunks, n_expert, capacity, piece)
    by_tensor = (chunks, n_tensor, tok_rows, piece)
    dma = pltpu.SemaphoreType.DMA
    hbm = pl.BlockSpec(memory_space=pltpu.HBM)
    vmem = pl.BlockSpec(memory_space=pltpu.VMEM)
    return pl.pallas_call(
        functools.partial(kernel, chunks, n_expert, n_tensor),
        out_shape=(pltpu.VMEM(hidden_grad.shape, BF16), pltpu.VMEM(tokens.shape, BF16)),
        in_specs=[hbm] * 7,
        out_specs=(vmem, vmem),
        scratch_shapes=[
            pltpu.VMEM(tokens.shape, BF16),
            pltpu.SMEM(expert_ids.shape, jnp.int32),
            pltpu.SMEM(slot_ids.shape, jnp.int32),
            pltpu.VMEM(router.shape[::-1], BF16),
            pltpu.VMEM(w_gate.shape[1:], BF16),
            pltpu.VMEM(w_up.shape[1:], BF16),
            pltpu.VMEM((slots, hidden), BF16),
            pltpu.VMEM((n_tensor, tok_rows, 128), jnp.int32),
            pltpu.VMEM(by_tensor, BF16),
            pltpu.VMEM(by_expert, BF16),
            pltpu.VMEM(by_expert, BF16),
            pltpu.VMEM(by_expert, BF16),
            pltpu.VMEM(by_expert, BF16),
            pltpu.VMEM(by_tensor, BF16),
            pltpu.VMEM(by_tensor, BF16),
            pltpu.VMEM((slots, hidden), F32),
            pltpu.VMEM((slots, hidden), F32),
            pltpu.VMEM((slots, hidden), BF16),
            pltpu.VMEM((slots, hidden), BF16),
            pltpu.VMEM(tokens.shape, F32),
            dma((5,)),
            dma((2, chunks)),
            dma((2, 1)),
            dma((2, chunks)),
            dma((2, chunks)),
            dma((2, chunks)),
            dma((2, chunks)),
        ],
        compiler_params=pltpu.CompilerParams(
            collective_id=0, has_side_effects=True, vmem_limit_bytes=56 * 1024 * 1024
        ),
        name="routed_experts",
    )(tokens, expert_ids, slot_ids, router.T, w_gate, w_up, hidden_grad)

def solution(mesh):
    in_specs = (
        P(("expert", "tensor"), None),
        P(("expert", "tensor")),
        P(("expert", "tensor")),
        P(),
        P("expert", None, "tensor"),
        P("expert", None, "tensor"),
        P("expert", None, "tensor"),
    )
    out_specs = (P("expert", None, "tensor"), P(("expert", "tensor"), None))
    return jax.shard_map(shards, mesh=mesh, in_specs=in_specs, out_specs=out_specs, check_vma=False)
```

```python
import functools

import jax
import jax.numpy as jnp
from jax import lax
from jax.experimental import pallas as pl
from jax.experimental.pallas import tpu as pltpu
from jax.sharding import PartitionSpec as P

MESH = pl.DeviceIdType.MESH
F32 = jnp.float32
BF16 = jnp.bfloat16
PARTS = 4
UNIT = 256


def each(count, body):
    if count <= 16:
        for index in range(count):
            body(index)
    else:

        def step(index, carry):
            body(index)
            return carry

        lax.fori_loop(0, count, step, 0)


def cut(width):
    units = width // UNIT
    bounds = [UNIT * ((2 * i * units + PARTS) // (2 * PARTS)) for i in range(PARTS)] + [width]
    return [(low, high - low) for low, high in zip(bounds, bounds[1:]) if high > low]


def kernel(
    spans,
    n_expert,
    n_tensor,
    tokens_hbm,
    expert_hbm,
    slot_hbm,
    router_hbm,
    gate_hbm,
    up_hbm,
    grad_hbm,
    act,
    out,
    tokens,
    expert_ids,
    slot_ids,
    router,
    w_gate,
    w_up,
    hidden_grad,
    ids,
    rows,
    sent,
    arrived,
    part,
    returned,
    mine,
    partials,
    acc_gate,
    acc_up,
    d_gate,
    d_lifted,
    d_rows,
    in_sem,
    w_sem,
    ids_sem,
    rows_sem,
    slots_sem,
    part_sem,
    mine_sem,
):
    me_e = lax.axis_index("expert")
    me_t = lax.axis_index("tensor")
    tok_rows, width = tokens.shape
    chunks = len(spans)
    capacity = arrived.shape[1]
    slots = n_expert * capacity
    group = n_tensor * tok_rows

    def span(c):
        return pl.ds(*spans[c])

    def wrap(index, count):
        return jnp.where(index >= count, index - count, index)

    if n_tensor <= 16:
        list_t = [wrap(me_t + k + 1, n_tensor) for k in range(n_tensor - 1)]
    if n_expert <= 16:
        list_e = [wrap(me_e + k + 1, n_expert) for k in range(n_expert - 1)]

    def peer_t(k):
        return list_t[k] if n_tensor <= 16 else wrap(me_t + k + 1, n_tensor)

    def peer_e(k):
        return list_e[k] if n_expert <= 16 else wrap(me_e + k + 1, n_expert)

    def over_t(src, dst, sems, index, peer):
        return pltpu.make_async_remote_copy(
            src_ref=src,
            dst_ref=dst,
            send_sem=sems.at[0, index],
            recv_sem=sems.at[1, index],
            device_id=(me_e, peer),
            device_id_type=MESH,
        )

    def over_e(src, dst, sems, index, peer):
        return pltpu.make_async_remote_copy(
            src_ref=src,
            dst_ref=dst,
            send_sem=sems.at[0, index],
            recv_sem=sems.at[1, index],
            device_id=(peer, me_t),
            device_id_type=MESH,
        )

    def await_all(sem, buffer, count, columns):
        whole = buffer.at[pl.ds(0, count), :, columns]
        pltpu.make_async_copy(whole, whole, sem).wait()

    def landed(buffer, sems, c, count):
        await_all(sems.at[1, c], buffer, count, span(c))

    def left(buffer, sems, c, count):
        await_all(sems.at[0, c], buffer, count, span(c))

    loads = [
        pltpu.make_async_copy(expert_hbm, expert_ids, in_sem.at[0]),
        pltpu.make_async_copy(slot_hbm, slot_ids, in_sem.at[1]),
        pltpu.make_async_copy(tokens_hbm, tokens, in_sem.at[2]),
        pltpu.make_async_copy(router_hbm, router, in_sem.at[3]),
        pltpu.make_async_copy(grad_hbm.at[0], hidden_grad, in_sem.at[4]),
    ]
    for load in loads[:4]:
        load.start()

    barrier = pltpu.get_barrier_semaphore()

    def greet_t(k):
        pl.semaphore_signal(
            barrier, inc=1, device_id=(me_e, peer_t(k)), device_id_type=MESH
        )

    def greet_e(k):
        pl.semaphore_signal(
            barrier, inc=1, device_id=(peer_e(k), me_t), device_id_type=MESH
        )

    each(n_tensor - 1, greet_t)
    each(n_expert - 1, greet_e)

    weight_loads = []
    for c in range(chunks):
        pair = (
            pltpu.make_async_copy(gate_hbm.at[0, span(c)], w_gate.at[span(c)], w_sem.at[0, c]),
            pltpu.make_async_copy(up_hbm.at[0, span(c)], w_up.at[span(c)], w_sem.at[1, c]),
        )
        weight_loads.append(pair)
        for load in pair:
            load.start()
    loads[4].start()

    loads[0].wait()
    loads[1].wait()
    row_index = lax.broadcasted_iota(jnp.int32, (tok_rows, 128), 0)
    expert_of = jnp.zeros((tok_rows, 128), jnp.int32)
    slot_of = jnp.zeros((tok_rows, 128), jnp.int32)
    for i in range(tok_rows):
        expert_of = jnp.where(row_index == i, expert_ids[i], expert_of)
        slot_of = jnp.where(row_index == i, slot_ids[i], slot_of)
    ids[me_t] = expert_of * capacity + slot_of
    picked = (
        expert_of[:, :1] == lax.broadcasted_iota(jnp.int32, (tok_rows, n_expert), 1)
    ).astype(F32)

    loads[2].wait()
    loads[3].wait()
    column = jnp.dot(picked.astype(BF16), router[...], preferred_element_type=F32)
    token_values = tokens[...].astype(F32)
    score = jax.nn.sigmoid(jnp.sum(token_values * column, axis=1, keepdims=True))
    routed = (score * token_values).astype(BF16)
    rows[me_t] = routed

    pl.semaphore_wait(barrier, n_tensor + n_expert - 2)

    def send_ids(k):
        over_t(ids.at[me_t], ids.at[me_t], ids_sem, 0, peer_t(k)).start()

    each(n_tensor - 1, send_ids)
    for c in range(chunks):

        mine_rows = rows.at[me_t, :, span(c)]

        def send_rows(k):
            over_t(mine_rows, mine_rows, rows_sem, c, peer_t(k)).start()

        each(n_tensor - 1, send_rows)

    await_all(ids_sem.at[1, 0], ids, n_tensor - 1, pl.ds(0, 128))
    target = ids[...].reshape(group, 128)[:, :1]
    place = (target == lax.broadcasted_iota(jnp.int32, (group, slots), 1)).astype(F32)
    place_t = place.T.astype(BF16)
    place = place.astype(BF16)

    def dispatch(c):
        landed(rows, rows_sem, c, n_tensor - 1)
        group_rows = rows[:, :, span(c)].astype(F32).reshape(group, spans[c][1]).astype(BF16)
        placed = jnp.dot(place_t, group_rows, preferred_element_type=F32)
        sent[:, :, span(c)] = placed.reshape(n_expert, capacity, spans[c][1]).astype(BF16)

        def send(k):
            peer = peer_e(k)
            over_e(sent.at[peer, :, span(c)], arrived.at[me_e, :, span(c)], slots_sem, c, peer).start()

        each(n_expert - 1, send)
        arrived[me_e, :, span(c)] = sent[me_e, :, span(c)]

    def project(c):
        landed(arrived, slots_sem, c, n_expert - 1)
        for load in weight_loads[c]:
            load.wait()
        lhs = arrived[:, :, span(c)].astype(F32).reshape(slots, spans[c][1]).astype(BF16)
        for total, weight in ((acc_gate, w_gate), (acc_up, w_up)):
            product = jnp.dot(lhs, weight[span(c)], preferred_element_type=F32)
            total[...] = product if c == 0 else total[...] + product

    for c in range(chunks):
        dispatch(c)
    for c in range(chunks):
        project(c)

    loads[4].wait()
    gate_proj = acc_gate[...]
    lifted = acc_up[...]
    cotangent = hidden_grad[...].astype(F32)
    sigma = jax.nn.sigmoid(gate_proj)
    silu = gate_proj * sigma
    slope = sigma * (1.0 + gate_proj * (1.0 - sigma))
    d_gate[...] = (cotangent * lifted * slope).astype(BF16)
    d_lifted[...] = (cotangent * silu).astype(BF16)
    act[0] = (silu * lifted).astype(BF16)

    contract = (((1,), (1,)), ((), ()))

    def pull_back(c):
        value = lax.dot_general(
            d_gate[...], w_gate[span(c)], contract, preferred_element_type=F32
        ) + lax.dot_general(d_lifted[...], w_up[span(c)], contract, preferred_element_type=F32)
        part[:, :, span(c)] = value.reshape(n_expert, capacity, spans[c][1]).astype(BF16)

        def send(k):
            peer = peer_e(k)
            over_e(part.at[peer, :, span(c)], returned.at[me_e, :, span(c)], part_sem, c, peer).start()

        each(n_expert - 1, send)
        returned[me_e, :, span(c)] = part[me_e, :, span(c)]

    def collect(c):
        landed(returned, part_sem, c, n_expert - 1)
        slot_rows = returned[:, :, span(c)].astype(F32).reshape(slots, spans[c][1]).astype(BF16)
        token_rows = jnp.dot(place, slot_rows, preferred_element_type=F32)
        mine[:, :, span(c)] = token_rows.reshape(n_tensor, tok_rows, spans[c][1]).astype(BF16)

        def send(k):
            peer = peer_t(k)
            over_t(mine.at[peer, :, span(c)], partials.at[me_t, :, span(c)], mine_sem, c, peer).start()

        each(n_tensor - 1, send)
        partials[me_t, :, span(c)] = mine[me_t, :, span(c)]

    def add_up(c):
        landed(partials, mine_sem, c, n_tensor - 1)
        summed = jnp.sum(partials[:, :, span(c)].astype(F32), axis=0).astype(BF16).astype(F32)
        d_rows[:, span(c)] = summed
        return jnp.sum(tokens[:, span(c)].astype(F32) * summed, axis=1, keepdims=True)

    inner = jnp.zeros((tok_rows, 1), F32)
    for c in range(chunks):
        pull_back(c)
    for c in range(chunks):
        collect(c)
    for c in range(chunks):
        inner = inner + add_up(c)

    gradient = score * d_rows[...] + (inner * score * (1.0 - score)) * column
    out[...] = gradient.astype(BF16)

    await_all(ids_sem.at[0, 0], ids, n_tensor - 1, pl.ds(0, 128))
    for c in range(chunks):
        left(rows, rows_sem, c, n_tensor - 1)
        left(sent, slots_sem, c, n_expert - 1)
        left(part, part_sem, c, n_expert - 1)
        left(mine, mine_sem, c, n_tensor - 1)


def shards(tokens, expert_ids, slot_ids, router, w_gate, w_up, hidden_grad):
    n_tensor = lax.axis_size("tensor")
    n_expert = lax.axis_size("expert")
    tok_rows, width = tokens.shape
    slots, hidden = hidden_grad.shape[1:]
    capacity = slots // n_expert
    spans = cut(width)
    chunks = len(spans)
    by_expert = (n_expert, capacity, width)
    by_tensor = (n_tensor, tok_rows, width)
    dma = pltpu.SemaphoreType.DMA
    hbm = pl.BlockSpec(memory_space=pltpu.HBM)
    vmem = pl.BlockSpec(memory_space=pltpu.VMEM)
    return pl.pallas_call(
        functools.partial(kernel, spans, n_expert, n_tensor),
        out_shape=(pltpu.VMEM(hidden_grad.shape, BF16), pltpu.VMEM(tokens.shape, BF16)),
        in_specs=[hbm] * 7,
        out_specs=(vmem, vmem),
        scratch_shapes=[
            pltpu.VMEM(tokens.shape, BF16),
            pltpu.SMEM(expert_ids.shape, jnp.int32),
            pltpu.SMEM(slot_ids.shape, jnp.int32),
            pltpu.VMEM(router.shape[::-1], BF16),
            pltpu.VMEM(w_gate.shape[1:], BF16),
            pltpu.VMEM(w_up.shape[1:], BF16),
            pltpu.VMEM((slots, hidden), BF16),
            pltpu.VMEM((n_tensor, tok_rows, 128), jnp.int32),
            pltpu.VMEM(by_tensor, BF16),
            pltpu.VMEM(by_expert, BF16),
            pltpu.VMEM(by_expert, BF16),
            pltpu.VMEM(by_expert, BF16),
            pltpu.VMEM(by_expert, BF16),
            pltpu.VMEM(by_tensor, BF16),
            pltpu.VMEM(by_tensor, BF16),
            pltpu.VMEM((slots, hidden), F32),
            pltpu.VMEM((slots, hidden), F32),
            pltpu.VMEM((slots, hidden), BF16),
            pltpu.VMEM((slots, hidden), BF16),
            pltpu.VMEM(tokens.shape, F32),
            dma((5,)),
            dma((2, chunks)),
            dma((2, 1)),
            dma((2, chunks)),
            dma((2, chunks)),
            dma((2, chunks)),
            dma((2, chunks)),
        ],
        compiler_params=pltpu.CompilerParams(
            collective_id=0, has_side_effects=True, vmem_limit_bytes=56 * 1024 * 1024
        ),
        name="routed_experts",
    )(tokens, expert_ids, slot_ids, router.T, w_gate, w_up, hidden_grad)

def solution(mesh):
    in_specs = (
        P(("expert", "tensor"), None),
        P(("expert", "tensor")),
        P(("expert", "tensor")),
        P(),
        P("expert", None, "tensor"),
        P("expert", None, "tensor"),
        P("expert", None, "tensor"),
    )
    out_specs = (P("expert", None, "tensor"), P(("expert", "tensor"), None))
    return jax.shard_map(shards, mesh=mesh, in_specs=in_specs, out_specs=out_specs, check_vma=False)
```

```python
import functools

import jax
import jax.numpy as jnp
from jax import lax
from jax.experimental import pallas as pl
from jax.experimental.pallas import tpu as pltpu
from jax.sharding import PartitionSpec as P

MESH = pl.DeviceIdType.MESH
F32 = jnp.float32
BF16 = jnp.bfloat16
PARTS = 3
UNIT = 256


def each(count, body):
    if count <= 16:
        for index in range(count):
            body(index)
    else:

        def step(index, carry):
            body(index)
            return carry

        lax.fori_loop(0, count, step, 0)


def cut(width):
    units = width // UNIT
    bounds = [UNIT * ((2 * i * units + PARTS) // (2 * PARTS)) for i in range(PARTS)] + [width]
    return [(low, high - low) for low, high in zip(bounds, bounds[1:]) if high > low]


def kernel(
    spans,
    n_expert,
    n_tensor,
    tokens_hbm,
    expert_hbm,
    slot_hbm,
    router_hbm,
    gate_hbm,
    up_hbm,
    grad_hbm,
    act,
    out,
    tokens,
    expert_ids,
    slot_ids,
    router,
    w_gate,
    w_up,
    hidden_grad,
    ids,
    rows,
    sent,
    arrived,
    part,
    returned,
    mine,
    partials,
    acc_gate,
    acc_up,
    d_gate,
    d_lifted,
    d_rows,
    in_sem,
    w_sem,
    ids_sem,
    rows_sem,
    slots_sem,
    part_sem,
    mine_sem,
):
    me_e = lax.axis_index("expert")
    me_t = lax.axis_index("tensor")
    tok_rows, width = tokens.shape
    chunks = len(spans)
    capacity = arrived.shape[1]
    slots = n_expert * capacity
    group = n_tensor * tok_rows

    def span(c):
        return pl.ds(*spans[c])

    def wrap(index, count):
        return jnp.where(index >= count, index - count, index)

    if n_tensor <= 16:
        list_t = [wrap(me_t + k + 1, n_tensor) for k in range(n_tensor - 1)]
    if n_expert <= 16:
        list_e = [wrap(me_e + k + 1, n_expert) for k in range(n_expert - 1)]

    def peer_t(k):
        return list_t[k] if n_tensor <= 16 else wrap(me_t + k + 1, n_tensor)

    def peer_e(k):
        return list_e[k] if n_expert <= 16 else wrap(me_e + k + 1, n_expert)

    def over_t(src, dst, sems, index, peer):
        return pltpu.make_async_remote_copy(
            src_ref=src,
            dst_ref=dst,
            send_sem=sems.at[0, index],
            recv_sem=sems.at[1, index],
            device_id=(me_e, peer),
            device_id_type=MESH,
        )

    def over_e(src, dst, sems, index, peer):
        return pltpu.make_async_remote_copy(
            src_ref=src,
            dst_ref=dst,
            send_sem=sems.at[0, index],
            recv_sem=sems.at[1, index],
            device_id=(peer, me_t),
            device_id_type=MESH,
        )

    def await_all(sem, buffer, count, columns):
        whole = buffer.at[pl.ds(0, count), :, columns]
        pltpu.make_async_copy(whole, whole, sem).wait()

    def landed(buffer, sems, c, count):
        await_all(sems.at[1, c], buffer, count, span(c))

    def left(buffer, sems, c, count):
        await_all(sems.at[0, c], buffer, count, span(c))

    loads = [
        pltpu.make_async_copy(expert_hbm, expert_ids, in_sem.at[0]),
        pltpu.make_async_copy(slot_hbm, slot_ids, in_sem.at[1]),
        pltpu.make_async_copy(tokens_hbm, tokens, in_sem.at[2]),
        pltpu.make_async_copy(router_hbm, router, in_sem.at[3]),
        pltpu.make_async_copy(grad_hbm.at[0], hidden_grad, in_sem.at[4]),
    ]
    for load in loads[:4]:
        load.start()

    barrier = pltpu.get_barrier_semaphore()

    def greet_t(k):
        pl.semaphore_signal(
            barrier, inc=1, device_id=(me_e, peer_t(k)), device_id_type=MESH
        )

    def greet_e(k):
        pl.semaphore_signal(
            barrier, inc=1, device_id=(peer_e(k), me_t), device_id_type=MESH
        )

    each(n_tensor - 1, greet_t)
    each(n_expert - 1, greet_e)

    weight_loads = []
    for c in range(chunks):
        pair = (
            pltpu.make_async_copy(gate_hbm.at[0, span(c)], w_gate.at[span(c)], w_sem.at[0, c]),
            pltpu.make_async_copy(up_hbm.at[0, span(c)], w_up.at[span(c)], w_sem.at[1, c]),
        )
        weight_loads.append(pair)
    for load in weight_loads[0]:
        load.start()

    loads[0].wait()
    loads[1].wait()
    row_index = lax.broadcasted_iota(jnp.int32, (tok_rows, 128), 0)
    expert_of = jnp.zeros((tok_rows, 128), jnp.int32)
    slot_of = jnp.zeros((tok_rows, 128), jnp.int32)
    for i in range(tok_rows):
        expert_of = jnp.where(row_index == i, expert_ids[i], expert_of)
        slot_of = jnp.where(row_index == i, slot_ids[i], slot_of)
    ids[me_t] = expert_of * capacity + slot_of
    picked = (
        expert_of[:, :1] == lax.broadcasted_iota(jnp.int32, (tok_rows, n_expert), 1)
    ).astype(F32)

    loads[2].wait()
    loads[3].wait()
    column = jnp.dot(picked.astype(BF16), router[...], preferred_element_type=F32)
    token_values = tokens[...].astype(F32)
    score = jax.nn.sigmoid(jnp.sum(token_values * column, axis=1, keepdims=True))
    routed = (score * token_values).astype(BF16)
    rows[me_t] = routed

    pl.semaphore_wait(barrier, n_tensor + n_expert - 2)

    def send_ids(k):
        over_t(ids.at[me_t], ids.at[me_t], ids_sem, 0, peer_t(k)).start()

    each(n_tensor - 1, send_ids)
    for c in range(chunks):

        mine_rows = rows.at[me_t, :, span(c)]

        def send_rows(k):
            over_t(mine_rows, mine_rows, rows_sem, c, peer_t(k)).start()

        each(n_tensor - 1, send_rows)

    for pair in weight_loads[1:]:
        for load in pair:
            load.start()
    loads[4].start()

    await_all(ids_sem.at[1, 0], ids, n_tensor - 1, pl.ds(0, 128))
    target = ids[...].reshape(group, 128)[:, :1]
    place = (target == lax.broadcasted_iota(jnp.int32, (group, slots), 1)).astype(F32)
    place_t = place.T.astype(BF16)
    place = place.astype(BF16)

    def dispatch(c):
        landed(rows, rows_sem, c, n_tensor - 1)
        group_rows = rows[:, :, span(c)].astype(F32).reshape(group, spans[c][1]).astype(BF16)
        placed = jnp.dot(place_t, group_rows, preferred_element_type=F32)
        sent[:, :, span(c)] = placed.reshape(n_expert, capacity, spans[c][1]).astype(BF16)

        def send(k):
            peer = peer_e(k)
            over_e(sent.at[peer, :, span(c)], arrived.at[me_e, :, span(c)], slots_sem, c, peer).start()

        each(n_expert - 1, send)
        arrived[me_e, :, span(c)] = sent[me_e, :, span(c)]

    def project(c):
        landed(arrived, slots_sem, c, n_expert - 1)
        for load in weight_loads[c]:
            load.wait()
        lhs = arrived[:, :, span(c)].astype(F32).reshape(slots, spans[c][1]).astype(BF16)
        for total, weight in ((acc_gate, w_gate), (acc_up, w_up)):
            product = jnp.dot(lhs, weight[span(c)], preferred_element_type=F32)
            total[...] = product if c == 0 else total[...] + product

    for c in range(chunks):
        dispatch(c)
    for c in range(chunks):
        project(c)

    loads[4].wait()
    gate_proj = acc_gate[...]
    lifted = acc_up[...]
    cotangent = hidden_grad[...].astype(F32)
    sigma = jax.nn.sigmoid(gate_proj)
    silu = gate_proj * sigma
    slope = sigma * (1.0 + gate_proj * (1.0 - sigma))
    d_gate[...] = (cotangent * lifted * slope).astype(BF16)
    d_lifted[...] = (cotangent * silu).astype(BF16)

    contract = (((1,), (1,)), ((), ()))

    def pull_back(c):
        value = lax.dot_general(
            d_gate[...], w_gate[span(c)], contract, preferred_element_type=F32
        ) + lax.dot_general(d_lifted[...], w_up[span(c)], contract, preferred_element_type=F32)
        part[:, :, span(c)] = value.reshape(n_expert, capacity, spans[c][1]).astype(BF16)

        def send(k):
            peer = peer_e(k)
            over_e(part.at[peer, :, span(c)], returned.at[me_e, :, span(c)], part_sem, c, peer).start()

        each(n_expert - 1, send)
        returned[me_e, :, span(c)] = part[me_e, :, span(c)]

    def collect(c):
        landed(returned, part_sem, c, n_expert - 1)
        slot_rows = returned[:, :, span(c)].astype(F32).reshape(slots, spans[c][1]).astype(BF16)
        token_rows = jnp.dot(place, slot_rows, preferred_element_type=F32)
        mine[:, :, span(c)] = token_rows.reshape(n_tensor, tok_rows, spans[c][1]).astype(BF16)

        def send(k):
            peer = peer_t(k)
            over_t(mine.at[peer, :, span(c)], partials.at[me_t, :, span(c)], mine_sem, c, peer).start()

        each(n_tensor - 1, send)
        partials[me_t, :, span(c)] = mine[me_t, :, span(c)]

    def add_up(c):
        landed(partials, mine_sem, c, n_tensor - 1)
        summed = jnp.sum(partials[:, :, span(c)].astype(F32), axis=0).astype(BF16).astype(F32)
        d_rows[:, span(c)] = summed
        return jnp.sum(tokens[:, span(c)].astype(F32) * summed, axis=1, keepdims=True)

    inner = jnp.zeros((tok_rows, 1), F32)
    for c in range(chunks):
        pull_back(c)
    gate_again = acc_gate[...]
    act[0] = (gate_again * jax.nn.sigmoid(gate_again) * acc_up[...]).astype(BF16)
    for c in range(chunks):
        collect(c)
    for c in range(chunks):
        inner = inner + add_up(c)

    gradient = score * d_rows[...] + (inner * score * (1.0 - score)) * column
    out[...] = gradient.astype(BF16)

    await_all(ids_sem.at[0, 0], ids, n_tensor - 1, pl.ds(0, 128))
    for c in range(chunks):
        left(rows, rows_sem, c, n_tensor - 1)
        left(sent, slots_sem, c, n_expert - 1)
        left(part, part_sem, c, n_expert - 1)
        left(mine, mine_sem, c, n_tensor - 1)


def shards(tokens, expert_ids, slot_ids, router, w_gate, w_up, hidden_grad):
    n_tensor = lax.axis_size("tensor")
    n_expert = lax.axis_size("expert")
    tok_rows, width = tokens.shape
    slots, hidden = hidden_grad.shape[1:]
    capacity = slots // n_expert
    spans = cut(width)
    chunks = len(spans)
    by_expert = (n_expert, capacity, width)
    by_tensor = (n_tensor, tok_rows, width)
    dma = pltpu.SemaphoreType.DMA
    hbm = pl.BlockSpec(memory_space=pltpu.HBM)
    vmem = pl.BlockSpec(memory_space=pltpu.VMEM)
    return pl.pallas_call(
        functools.partial(kernel, spans, n_expert, n_tensor),
        out_shape=(pltpu.VMEM(hidden_grad.shape, BF16), pltpu.VMEM(tokens.shape, BF16)),
        in_specs=[hbm] * 7,
        out_specs=(vmem, vmem),
        scratch_shapes=[
            pltpu.VMEM(tokens.shape, BF16),
            pltpu.SMEM(expert_ids.shape, jnp.int32),
            pltpu.SMEM(slot_ids.shape, jnp.int32),
            pltpu.VMEM(router.shape[::-1], BF16),
            pltpu.VMEM(w_gate.shape[1:], BF16),
            pltpu.VMEM(w_up.shape[1:], BF16),
            pltpu.VMEM((slots, hidden), BF16),
            pltpu.VMEM((n_tensor, tok_rows, 128), jnp.int32),
            pltpu.VMEM(by_tensor, BF16),
            pltpu.VMEM(by_expert, BF16),
            pltpu.VMEM(by_expert, BF16),
            pltpu.VMEM(by_expert, BF16),
            pltpu.VMEM(by_expert, BF16),
            pltpu.VMEM(by_tensor, BF16),
            pltpu.VMEM(by_tensor, BF16),
            pltpu.VMEM((slots, hidden), F32),
            pltpu.VMEM((slots, hidden), F32),
            pltpu.VMEM((slots, hidden), BF16),
            pltpu.VMEM((slots, hidden), BF16),
            pltpu.VMEM(tokens.shape, F32),
            dma((5,)),
            dma((2, chunks)),
            dma((2, 1)),
            dma((2, chunks)),
            dma((2, chunks)),
            dma((2, chunks)),
            dma((2, chunks)),
        ],
        compiler_params=pltpu.CompilerParams(
            collective_id=0, has_side_effects=True, vmem_limit_bytes=56 * 1024 * 1024
        ),
        name="routed_experts",
    )(tokens, expert_ids, slot_ids, router.T, w_gate, w_up, hidden_grad)

def solution(mesh):
    in_specs = (
        P(("expert", "tensor"), None),
        P(("expert", "tensor")),
        P(("expert", "tensor")),
        P(),
        P("expert", None, "tensor"),
        P("expert", None, "tensor"),
        P("expert", None, "tensor"),
    )
    out_specs = (P("expert", None, "tensor"), P(("expert", "tensor"), None))
    return jax.shard_map(shards, mesh=mesh, in_specs=in_specs, out_specs=out_specs, check_vma=False)
```

```python
import functools

import jax
import jax.numpy as jnp
from jax import lax
from jax.experimental import pallas as pl
from jax.experimental.pallas import tpu as pltpu
from jax.sharding import PartitionSpec as P

MESH = pl.DeviceIdType.MESH
F32 = jnp.float32
BF16 = jnp.bfloat16
PARTS = 3
UNIT = 256


def each(count, body):
    if count <= 16:
        for index in range(count):
            body(index)
    else:

        def step(index, carry):
            body(index)
            return carry

        lax.fori_loop(0, count, step, 0)


def cut(width):
    units = width // UNIT
    bounds = [UNIT * ((2 * i * units + PARTS) // (2 * PARTS)) for i in range(PARTS)] + [width]
    return [(low, high - low) for low, high in zip(bounds, bounds[1:]) if high > low]


def kernel(
    spans,
    n_expert,
    n_tensor,
    tokens_hbm,
    expert_hbm,
    slot_hbm,
    router_hbm,
    gate_hbm,
    up_hbm,
    grad_hbm,
    act,
    out,
    tokens,
    expert_ids,
    slot_ids,
    router,
    w_gate,
    w_up,
    hidden_grad,
    ids,
    rows,
    sent,
    arrived,
    part,
    returned,
    mine,
    partials,
    acc_gate,
    acc_up,
    d_gate,
    d_lifted,
    d_rows,
    in_sem,
    w_sem,
    ids_sem,
    rows_sem,
    slots_sem,
    part_sem,
    mine_sem,
):
    me_e = lax.axis_index("expert")
    me_t = lax.axis_index("tensor")
    tok_rows, width = tokens.shape
    chunks = len(spans)
    capacity = arrived.shape[1]
    slots = n_expert * capacity
    group = n_tensor * tok_rows

    def span(c):
        return pl.ds(*spans[c])

    def wrap(index, count):
        return jnp.where(index >= count, index - count, index)

    if n_tensor <= 16:
        list_t = [wrap(me_t + k + 1, n_tensor) for k in range(n_tensor - 1)]
    if n_expert <= 16:
        list_e = [wrap(me_e + k + 1, n_expert) for k in range(n_expert - 1)]

    def peer_t(k):
        return list_t[k] if n_tensor <= 16 else wrap(me_t + k + 1, n_tensor)

    def peer_e(k):
        return list_e[k] if n_expert <= 16 else wrap(me_e + k + 1, n_expert)

    def over_t(src, dst, sems, index, peer):
        return pltpu.make_async_remote_copy(
            src_ref=src,
            dst_ref=dst,
            send_sem=sems.at[0, index],
            recv_sem=sems.at[1, index],
            device_id=(me_e, peer),
            device_id_type=MESH,
        )

    def over_e(src, dst, sems, index, peer):
        return pltpu.make_async_remote_copy(
            src_ref=src,
            dst_ref=dst,
            send_sem=sems.at[0, index],
            recv_sem=sems.at[1, index],
            device_id=(peer, me_t),
            device_id_type=MESH,
        )

    def await_all(sem, buffer, count, columns):
        whole = buffer.at[pl.ds(0, count), :, columns]
        pltpu.make_async_copy(whole, whole, sem).wait()

    def landed(buffer, sems, c, count):
        await_all(sems.at[1, c], buffer, count, span(c))

    def left(buffer, sems, c, count):
        await_all(sems.at[0, c], buffer, count, span(c))

    loads = [
        pltpu.make_async_copy(expert_hbm, expert_ids, in_sem.at[0]),
        pltpu.make_async_copy(slot_hbm, slot_ids, in_sem.at[1]),
        pltpu.make_async_copy(tokens_hbm, tokens, in_sem.at[2]),
        pltpu.make_async_copy(router_hbm, router, in_sem.at[3]),
        pltpu.make_async_copy(grad_hbm.at[0], hidden_grad, in_sem.at[4]),
    ]
    for load in loads[:4]:
        load.start()

    barrier = pltpu.get_barrier_semaphore()

    def greet_t(k):
        pl.semaphore_signal(
            barrier, inc=1, device_id=(me_e, peer_t(k)), device_id_type=MESH
        )

    def greet_e(k):
        pl.semaphore_signal(
            barrier, inc=1, device_id=(peer_e(k), me_t), device_id_type=MESH
        )

    each(n_tensor - 1, greet_t)
    each(n_expert - 1, greet_e)

    weight_loads = []
    for c in range(chunks):
        pair = (
            pltpu.make_async_copy(gate_hbm.at[0, span(c)], w_gate.at[span(c)], w_sem.at[0, c]),
            pltpu.make_async_copy(up_hbm.at[0, span(c)], w_up.at[span(c)], w_sem.at[1, c]),
        )
        weight_loads.append(pair)
    for load in weight_loads[0]:
        load.start()

    loads[0].wait()
    loads[1].wait()
    row_index = lax.broadcasted_iota(jnp.int32, (tok_rows, 128), 0)
    expert_of = jnp.zeros((tok_rows, 128), jnp.int32)
    slot_of = jnp.zeros((tok_rows, 128), jnp.int32)
    for i in range(tok_rows):
        expert_of = jnp.where(row_index == i, expert_ids[i], expert_of)
        slot_of = jnp.where(row_index == i, slot_ids[i], slot_of)
    ids[me_t] = expert_of * capacity + slot_of
    picked = (
        expert_of[:, :1] == lax.broadcasted_iota(jnp.int32, (tok_rows, n_expert), 1)
    ).astype(F32)

    loads[2].wait()
    loads[3].wait()
    column = jnp.dot(picked.astype(BF16), router[...], preferred_element_type=F32)
    token_values = tokens[...].astype(F32)
    score = jax.nn.sigmoid(jnp.sum(token_values * column, axis=1, keepdims=True))
    routed = (score * token_values).astype(BF16)
    rows[me_t] = routed

    pl.semaphore_wait(barrier, n_tensor + n_expert - 2)

    def send_ids(k):
        over_t(ids.at[me_t], ids.at[me_t], ids_sem, 0, peer_t(k)).start()

    each(n_tensor - 1, send_ids)
    for c in range(chunks):

        mine_rows = rows.at[me_t, :, span(c)]

        def send_rows(k):
            over_t(mine_rows, mine_rows, rows_sem, c, peer_t(k)).start()

        each(n_tensor - 1, send_rows)

    for pair in weight_loads[1:]:
        for load in pair:
            load.start()
    loads[4].start()

    await_all(ids_sem.at[1, 0], ids, n_tensor - 1, pl.ds(0, 128))
    target = ids[...].reshape(group, 128)[:, :1]
    place = (target == lax.broadcasted_iota(jnp.int32, (group, slots), 1)).astype(F32)
    place_t = place.T.astype(BF16)
    place = place.astype(BF16)

    def dispatch(c):
        landed(rows, rows_sem, c, n_tensor - 1)
        group_rows = rows[:, :, span(c)].astype(F32).reshape(group, spans[c][1]).astype(BF16)
        placed = jnp.dot(place_t, group_rows, preferred_element_type=F32)
        sent[:, :, span(c)] = placed.reshape(n_expert, capacity, spans[c][1]).astype(BF16)

        def send(k):
            peer = peer_e(k)
            over_e(sent.at[peer, :, span(c)], arrived.at[me_e, :, span(c)], slots_sem, c, peer).start()

        each(n_expert - 1, send)
        arrived[me_e, :, span(c)] = sent[me_e, :, span(c)]

    def project(c):
        landed(arrived, slots_sem, c, n_expert - 1)
        for load in weight_loads[c]:
            load.wait()
        lhs = arrived[:, :, span(c)].astype(F32).reshape(slots, spans[c][1]).astype(BF16)
        for total, weight in ((acc_gate, w_gate), (acc_up, w_up)):
            product = jnp.dot(lhs, weight[span(c)], preferred_element_type=F32)
            total[...] = product if c == 0 else total[...] + product

    for c in range(chunks):
        dispatch(c)
    for c in range(chunks):
        project(c)

    loads[4].wait()
    gate_proj = acc_gate[...]
    lifted = acc_up[...]
    cotangent = hidden_grad[...].astype(F32)
    sigma = jax.nn.sigmoid(gate_proj)
    silu = gate_proj * sigma
    slope = sigma * (1.0 + gate_proj * (1.0 - sigma))
    d_gate[...] = (cotangent * lifted * slope).T.astype(BF16)
    d_lifted[...] = (cotangent * silu).T.astype(BF16)

    def pull_back(c):
        value = jnp.dot(w_gate[span(c)], d_gate[...], preferred_element_type=F32)
        value = value + jnp.dot(w_up[span(c)], d_lifted[...], preferred_element_type=F32)
        value = value.T
        part[:, :, span(c)] = value.reshape(n_expert, capacity, spans[c][1]).astype(BF16)

        def send(k):
            peer = peer_e(k)
            over_e(part.at[peer, :, span(c)], returned.at[me_e, :, span(c)], part_sem, c, peer).start()

        each(n_expert - 1, send)
        returned[me_e, :, span(c)] = part[me_e, :, span(c)]

    def collect(c):
        landed(returned, part_sem, c, n_expert - 1)
        slot_rows = returned[:, :, span(c)].astype(F32).reshape(slots, spans[c][1]).astype(BF16)
        token_rows = jnp.dot(place, slot_rows, preferred_element_type=F32)
        mine[:, :, span(c)] = token_rows.reshape(n_tensor, tok_rows, spans[c][1]).astype(BF16)

        def send(k):
            peer = peer_t(k)
            over_t(mine.at[peer, :, span(c)], partials.at[me_t, :, span(c)], mine_sem, c, peer).start()

        each(n_tensor - 1, send)
        partials[me_t, :, span(c)] = mine[me_t, :, span(c)]

    def add_up(c):
        landed(partials, mine_sem, c, n_tensor - 1)
        summed = jnp.sum(partials[:, :, span(c)].astype(F32), axis=0).astype(BF16).astype(F32)
        d_rows[:, span(c)] = summed
        return jnp.sum(tokens[:, span(c)].astype(F32) * summed, axis=1, keepdims=True)

    inner = jnp.zeros((tok_rows, 1), F32)
    for c in range(chunks):
        pull_back(c)
    gate_again = acc_gate[...]
    act[0] = (gate_again * jax.nn.sigmoid(gate_again) * acc_up[...]).astype(BF16)
    for c in range(chunks):
        collect(c)
    for c in range(chunks):
        inner = inner + add_up(c)

    gradient = score * d_rows[...] + (inner * score * (1.0 - score)) * column
    out[...] = gradient.astype(BF16)

    await_all(ids_sem.at[0, 0], ids, n_tensor - 1, pl.ds(0, 128))
    for c in range(chunks):
        left(rows, rows_sem, c, n_tensor - 1)
        left(sent, slots_sem, c, n_expert - 1)
        left(part, part_sem, c, n_expert - 1)
        left(mine, mine_sem, c, n_tensor - 1)


def shards(tokens, expert_ids, slot_ids, router, w_gate, w_up, hidden_grad):
    n_tensor = lax.axis_size("tensor")
    n_expert = lax.axis_size("expert")
    tok_rows, width = tokens.shape
    slots, hidden = hidden_grad.shape[1:]
    capacity = slots // n_expert
    spans = cut(width)
    chunks = len(spans)
    by_expert = (n_expert, capacity, width)
    by_tensor = (n_tensor, tok_rows, width)
    dma = pltpu.SemaphoreType.DMA
    hbm = pl.BlockSpec(memory_space=pltpu.HBM)
    vmem = pl.BlockSpec(memory_space=pltpu.VMEM)
    return pl.pallas_call(
        functools.partial(kernel, spans, n_expert, n_tensor),
        out_shape=(pltpu.VMEM(hidden_grad.shape, BF16), pltpu.VMEM(tokens.shape, BF16)),
        in_specs=[hbm] * 7,
        out_specs=(vmem, vmem),
        scratch_shapes=[
            pltpu.VMEM(tokens.shape, BF16),
            pltpu.SMEM(expert_ids.shape, jnp.int32),
            pltpu.SMEM(slot_ids.shape, jnp.int32),
            pltpu.VMEM(router.shape[::-1], BF16),
            pltpu.VMEM(w_gate.shape[1:], BF16),
            pltpu.VMEM(w_up.shape[1:], BF16),
            pltpu.VMEM((slots, hidden), BF16),
            pltpu.VMEM((n_tensor, tok_rows, 128), jnp.int32),
            pltpu.VMEM(by_tensor, BF16),
            pltpu.VMEM(by_expert, BF16),
            pltpu.VMEM(by_expert, BF16),
            pltpu.VMEM(by_expert, BF16),
            pltpu.VMEM(by_expert, BF16),
            pltpu.VMEM(by_tensor, BF16),
            pltpu.VMEM(by_tensor, BF16),
            pltpu.VMEM((slots, hidden), F32),
            pltpu.VMEM((slots, hidden), F32),
            pltpu.VMEM((hidden, slots), BF16),
            pltpu.VMEM((hidden, slots), BF16),
            pltpu.VMEM(tokens.shape, F32),
            dma((5,)),
            dma((2, chunks)),
            dma((2, 1)),
            dma((2, chunks)),
            dma((2, chunks)),
            dma((2, chunks)),
            dma((2, chunks)),
        ],
        compiler_params=pltpu.CompilerParams(
            collective_id=0, has_side_effects=True, vmem_limit_bytes=56 * 1024 * 1024
        ),
        name="routed_experts",
    )(tokens, expert_ids, slot_ids, router.T, w_gate, w_up, hidden_grad)

def solution(mesh):
    in_specs = (
        P(("expert", "tensor"), None),
        P(("expert", "tensor")),
        P(("expert", "tensor")),
        P(),
        P("expert", None, "tensor"),
        P("expert", None, "tensor"),
        P("expert", None, "tensor"),
    )
    out_specs = (P("expert", None, "tensor"), P(("expert", "tensor"), None))
    return jax.shard_map(shards, mesh=mesh, in_specs=in_specs, out_specs=out_specs, check_vma=False)
```

```python
import functools

import jax
import jax.numpy as jnp
from jax import lax
from jax.experimental import pallas as pl
from jax.experimental.pallas import tpu as pltpu
from jax.sharding import PartitionSpec as P

MESH = pl.DeviceIdType.MESH
F32 = jnp.float32
BF16 = jnp.bfloat16
PARTS = 3
UNIT = 256


def each(count, body):
    if count <= 16:
        for index in range(count):
            body(index)
    else:

        def step(index, carry):
            body(index)
            return carry

        lax.fori_loop(0, count, step, 0)


def cut(width):
    units = width // UNIT
    bounds = [UNIT * ((2 * i * units + PARTS) // (2 * PARTS)) for i in range(PARTS)] + [width]
    return [(low, high - low) for low, high in zip(bounds, bounds[1:]) if high > low]


def kernel(
    spans,
    n_expert,
    n_tensor,
    tokens_hbm,
    expert_hbm,
    slot_hbm,
    router_hbm,
    gate_hbm,
    up_hbm,
    grad_hbm,
    act,
    out,
    expert_ids,
    slot_ids,
    router,
    w_gate,
    w_up,
    hidden_grad,
    ids,
    scores,
    rows,
    sent,
    arrived,
    part,
    returned,
    mine,
    partials,
    acc_gate,
    acc_up,
    d_gate,
    d_lifted,
    d_rows,
    in_sem,
    w_sem,
    ids_sem,
    scores_sem,
    rows_sem,
    slots_sem,
    part_sem,
    mine_sem,
):
    me_e = lax.axis_index("expert")
    me_t = lax.axis_index("tensor")
    tok_rows, width = out.shape
    chunks = len(spans)
    capacity = arrived.shape[1]
    slots = n_expert * capacity
    group = n_tensor * tok_rows

    def span(c):
        return pl.ds(*spans[c])

    def wrap(index, count):
        return jnp.where(index >= count, index - count, index)

    if n_tensor <= 16:
        list_t = [wrap(me_t + k + 1, n_tensor) for k in range(n_tensor - 1)]
    if n_expert <= 16:
        list_e = [wrap(me_e + k + 1, n_expert) for k in range(n_expert - 1)]

    def peer_t(k):
        return list_t[k] if n_tensor <= 16 else wrap(me_t + k + 1, n_tensor)

    def peer_e(k):
        return list_e[k] if n_expert <= 16 else wrap(me_e + k + 1, n_expert)

    def over_t(src, dst, sems, index, peer):
        return pltpu.make_async_remote_copy(
            src_ref=src,
            dst_ref=dst,
            send_sem=sems.at[0, index],
            recv_sem=sems.at[1, index],
            device_id=(me_e, peer),
            device_id_type=MESH,
        )

    def over_e(src, dst, sems, index, peer):
        return pltpu.make_async_remote_copy(
            src_ref=src,
            dst_ref=dst,
            send_sem=sems.at[0, index],
            recv_sem=sems.at[1, index],
            device_id=(peer, me_t),
            device_id_type=MESH,
        )

    def await_all(sem, buffer, count, columns):
        whole = buffer.at[pl.ds(0, count), :, columns]
        pltpu.make_async_copy(whole, whole, sem).wait()

    def landed(buffer, sems, c, count):
        await_all(sems.at[1, c], buffer, count, span(c))

    def left(buffer, sems, c, count):
        await_all(sems.at[0, c], buffer, count, span(c))

    loads = [
        pltpu.make_async_copy(expert_hbm, expert_ids, in_sem.at[0]),
        pltpu.make_async_copy(slot_hbm, slot_ids, in_sem.at[1]),
        pltpu.make_async_copy(tokens_hbm, rows.at[me_t], in_sem.at[2]),
        pltpu.make_async_copy(router_hbm, router, in_sem.at[3]),
        pltpu.make_async_copy(grad_hbm.at[0], hidden_grad, in_sem.at[4]),
    ]
    for load in loads[:4]:
        load.start()

    barrier = pltpu.get_barrier_semaphore()

    def greet_t(k):
        pl.semaphore_signal(
            barrier, inc=1, device_id=(me_e, peer_t(k)), device_id_type=MESH
        )

    def greet_e(k):
        pl.semaphore_signal(
            barrier, inc=1, device_id=(peer_e(k), me_t), device_id_type=MESH
        )

    each(n_tensor - 1, greet_t)
    each(n_expert - 1, greet_e)

    weight_loads = []
    for c in range(chunks):
        pair = (
            pltpu.make_async_copy(gate_hbm.at[0, span(c)], w_gate.at[span(c)], w_sem.at[0, c]),
            pltpu.make_async_copy(up_hbm.at[0, span(c)], w_up.at[span(c)], w_sem.at[1, c]),
        )
        weight_loads.append(pair)
    for load in weight_loads[0]:
        load.start()

    def send_rows(c):
        mine_rows = rows.at[me_t, :, span(c)]
        each(
            n_tensor - 1,
            lambda k: over_t(mine_rows, mine_rows, rows_sem, c, peer_t(k)).start(),
        )

    loads[2].wait()
    pl.semaphore_wait(barrier, n_tensor + n_expert - 2)
    send_rows(0)

    loads[0].wait()
    loads[1].wait()
    row_index = lax.broadcasted_iota(jnp.int32, (tok_rows, 128), 0)
    expert_of = jnp.zeros((tok_rows, 128), jnp.int32)
    slot_of = jnp.zeros((tok_rows, 128), jnp.int32)
    for i in range(tok_rows):
        expert_of = jnp.where(row_index == i, expert_ids[i], expert_of)
        slot_of = jnp.where(row_index == i, slot_ids[i], slot_of)
    ids[me_t] = expert_of * capacity + slot_of
    picked = (
        expert_of[:, :1] == lax.broadcasted_iota(jnp.int32, (tok_rows, n_expert), 1)
    ).astype(F32)

    loads[3].wait()
    column = jnp.dot(picked.astype(BF16), router[...], preferred_element_type=F32)
    token_values = rows[me_t].astype(F32)
    score = jax.nn.sigmoid(jnp.sum(token_values * column, axis=1, keepdims=True))
    scores[me_t] = jnp.broadcast_to(score, (tok_rows, 128))

    def send_ids(k):
        over_t(ids.at[me_t], ids.at[me_t], ids_sem, 0, peer_t(k)).start()
        over_t(scores.at[me_t], scores.at[me_t], scores_sem, 0, peer_t(k)).start()

    each(n_tensor - 1, send_ids)
    for c in range(1, chunks):
        send_rows(c)

    for pair in weight_loads[1:]:
        for load in pair:
            load.start()
    loads[4].start()

    await_all(ids_sem.at[1, 0], ids, n_tensor - 1, pl.ds(0, 128))
    await_all(scores_sem.at[1, 0], scores, n_tensor - 1, pl.ds(0, 128))
    target = ids[...].reshape(group, 128)[:, :1]
    group_score = scores[...].reshape(group, 128)[:, :1]
    place = (target == lax.broadcasted_iota(jnp.int32, (group, slots), 1)).astype(F32)
    place_t = place.T.astype(BF16)
    place = place.astype(BF16)

    def dispatch(c):
        landed(rows, rows_sem, c, n_tensor - 1)
        raw_rows = rows[:, :, span(c)].astype(F32).reshape(group, spans[c][1])
        group_rows = (group_score * raw_rows).astype(BF16)
        placed = jnp.dot(place_t, group_rows, preferred_element_type=F32)
        sent[:, :, span(c)] = placed.reshape(n_expert, capacity, spans[c][1]).astype(BF16)

        def send(k):
            peer = peer_e(k)
            over_e(sent.at[peer, :, span(c)], arrived.at[me_e, :, span(c)], slots_sem, c, peer).start()

        each(n_expert - 1, send)
        arrived[me_e, :, span(c)] = sent[me_e, :, span(c)]

    def project(c):
        landed(arrived, slots_sem, c, n_expert - 1)
        for load in weight_loads[c]:
            load.wait()
        lhs = arrived[:, :, span(c)].astype(F32).reshape(slots, spans[c][1]).astype(BF16)
        for total, weight in ((acc_gate, w_gate), (acc_up, w_up)):
            product = jnp.dot(lhs, weight[span(c)], preferred_element_type=F32)
            total[...] = product if c == 0 else total[...] + product

    for c in range(chunks):
        dispatch(c)
    for c in range(chunks):
        project(c)

    loads[4].wait()
    gate_proj = acc_gate[...]
    lifted = acc_up[...]
    cotangent = hidden_grad[...].astype(F32)
    sigma = jax.nn.sigmoid(gate_proj)
    silu = gate_proj * sigma
    slope = sigma * (1.0 + gate_proj * (1.0 - sigma))
    d_gate[...] = (cotangent * lifted * slope).astype(BF16)
    d_lifted[...] = (cotangent * silu).astype(BF16)

    contract = (((1,), (1,)), ((), ()))

    def pull_back(c):
        value = lax.dot_general(
            d_gate[...], w_gate[span(c)], contract, preferred_element_type=F32
        ) + lax.dot_general(d_lifted[...], w_up[span(c)], contract, preferred_element_type=F32)
        part[:, :, span(c)] = value.reshape(n_expert, capacity, spans[c][1]).astype(BF16)

        def send(k):
            peer = peer_e(k)
            over_e(part.at[peer, :, span(c)], returned.at[me_e, :, span(c)], part_sem, c, peer).start()

        each(n_expert - 1, send)
        returned[me_e, :, span(c)] = part[me_e, :, span(c)]

    def collect(c):
        landed(returned, part_sem, c, n_expert - 1)
        slot_rows = returned[:, :, span(c)].astype(F32).reshape(slots, spans[c][1]).astype(BF16)
        token_rows = jnp.dot(place, slot_rows, preferred_element_type=F32)
        mine[:, :, span(c)] = token_rows.reshape(n_tensor, tok_rows, spans[c][1]).astype(BF16)

        def send(k):
            peer = peer_t(k)
            over_t(mine.at[peer, :, span(c)], partials.at[me_t, :, span(c)], mine_sem, c, peer).start()

        each(n_tensor - 1, send)
        partials[me_t, :, span(c)] = mine[me_t, :, span(c)]

    def add_up(c):
        landed(partials, mine_sem, c, n_tensor - 1)
        summed = jnp.sum(partials[:, :, span(c)].astype(F32), axis=0).astype(BF16).astype(F32)
        d_rows[:, span(c)] = summed
        return jnp.sum(rows[me_t, :, span(c)].astype(F32) * summed, axis=1, keepdims=True)

    inner = jnp.zeros((tok_rows, 1), F32)
    for c in range(chunks):
        pull_back(c)
    gate_again = acc_gate[...]
    act[0] = (gate_again * jax.nn.sigmoid(gate_again) * acc_up[...]).astype(BF16)
    for c in range(chunks):
        collect(c)
    for c in range(chunks):
        inner = inner + add_up(c)

    gradient = score * d_rows[...] + (inner * score * (1.0 - score)) * column
    out[...] = gradient.astype(BF16)

    await_all(ids_sem.at[0, 0], ids, n_tensor - 1, pl.ds(0, 128))
    await_all(scores_sem.at[0, 0], scores, n_tensor - 1, pl.ds(0, 128))
    for c in range(chunks):
        left(rows, rows_sem, c, n_tensor - 1)
        left(sent, slots_sem, c, n_expert - 1)
        left(part, part_sem, c, n_expert - 1)
        left(mine, mine_sem, c, n_tensor - 1)


def shards(tokens, expert_ids, slot_ids, router, w_gate, w_up, hidden_grad):
    n_tensor = lax.axis_size("tensor")
    n_expert = lax.axis_size("expert")
    tok_rows, width = tokens.shape
    slots, hidden = hidden_grad.shape[1:]
    capacity = slots // n_expert
    spans = cut(width)
    chunks = len(spans)
    by_expert = (n_expert, capacity, width)
    by_tensor = (n_tensor, tok_rows, width)
    dma = pltpu.SemaphoreType.DMA
    hbm = pl.BlockSpec(memory_space=pltpu.HBM)
    vmem = pl.BlockSpec(memory_space=pltpu.VMEM)
    return pl.pallas_call(
        functools.partial(kernel, spans, n_expert, n_tensor),
        out_shape=(pltpu.VMEM(hidden_grad.shape, BF16), pltpu.VMEM(tokens.shape, BF16)),
        in_specs=[hbm] * 7,
        out_specs=(vmem, vmem),
        scratch_shapes=[
            pltpu.SMEM(expert_ids.shape, jnp.int32),
            pltpu.SMEM(slot_ids.shape, jnp.int32),
            pltpu.VMEM(router.shape[::-1], BF16),
            pltpu.VMEM(w_gate.shape[1:], BF16),
            pltpu.VMEM(w_up.shape[1:], BF16),
            pltpu.VMEM((slots, hidden), BF16),
            pltpu.VMEM((n_tensor, tok_rows, 128), jnp.int32),
            pltpu.VMEM((n_tensor, tok_rows, 128), F32),
            pltpu.VMEM(by_tensor, BF16),
            pltpu.VMEM(by_expert, BF16),
            pltpu.VMEM(by_expert, BF16),
            pltpu.VMEM(by_expert, BF16),
            pltpu.VMEM(by_expert, BF16),
            pltpu.VMEM(by_tensor, BF16),
            pltpu.VMEM(by_tensor, BF16),
            pltpu.VMEM((slots, hidden), F32),
            pltpu.VMEM((slots, hidden), F32),
            pltpu.VMEM((slots, hidden), BF16),
            pltpu.VMEM((slots, hidden), BF16),
            pltpu.VMEM(tokens.shape, F32),
            dma((5,)),
            dma((2, chunks)),
            dma((2, 1)),
            dma((2, 1)),
            dma((2, chunks)),
            dma((2, chunks)),
            dma((2, chunks)),
            dma((2, chunks)),
        ],
        compiler_params=pltpu.CompilerParams(
            collective_id=0, has_side_effects=True, vmem_limit_bytes=56 * 1024 * 1024
        ),
        name="routed_experts",
    )(tokens, expert_ids, slot_ids, router.T, w_gate, w_up, hidden_grad)

def solution(mesh):
    in_specs = (
        P(("expert", "tensor"), None),
        P(("expert", "tensor")),
        P(("expert", "tensor")),
        P(),
        P("expert", None, "tensor"),
        P("expert", None, "tensor"),
        P("expert", None, "tensor"),
    )
    out_specs = (P("expert", None, "tensor"), P(("expert", "tensor"), None))
    return jax.shard_map(shards, mesh=mesh, in_specs=in_specs, out_specs=out_specs, check_vma=False)
```

```python
import functools

import jax
import jax.numpy as jnp
from jax import lax
from jax.experimental import pallas as pl
from jax.experimental.pallas import tpu as pltpu
from jax.sharding import PartitionSpec as P

MESH = pl.DeviceIdType.MESH
F32 = jnp.float32
BF16 = jnp.bfloat16
PARTS = 3
UNIT = 256


def each(count, body):
    if count <= 16:
        for index in range(count):
            body(index)
    else:

        def step(index, carry):
            body(index)
            return carry

        lax.fori_loop(0, count, step, 0)


def cut(width):
    units = width // UNIT
    bounds = [UNIT * ((2 * i * units + PARTS) // (2 * PARTS)) for i in range(PARTS)] + [width]
    return [(low, high - low) for low, high in zip(bounds, bounds[1:]) if high > low]


def kernel(
    spans,
    n_expert,
    n_tensor,
    tokens_hbm,
    expert_hbm,
    slot_hbm,
    router_hbm,
    gate_hbm,
    up_hbm,
    grad_hbm,
    act,
    out,
    tokens,
    expert_ids,
    slot_ids,
    router,
    w_gate,
    w_up,
    hidden_grad,
    ids,
    rows,
    sent,
    arrived,
    part,
    returned,
    mine,
    partials,
    acc_gate,
    acc_up,
    d_gate,
    d_lifted,
    d_rows,
    in_sem,
    w_sem,
    ids_sem,
    rows_sem,
    slots_sem,
    part_sem,
    mine_sem,
):
    me_e = lax.axis_index("expert")
    me_t = lax.axis_index("tensor")
    tok_rows, width = tokens.shape
    chunks = len(spans)
    capacity = arrived.shape[1]
    slots = n_expert * capacity
    group = n_tensor * tok_rows

    def span(c):
        return pl.ds(*spans[c])

    def wrap(index, count):
        return jnp.where(index >= count, index - count, index)

    if n_tensor <= 16:
        list_t = [wrap(me_t + k + 1, n_tensor) for k in range(n_tensor - 1)]
    if n_expert <= 16:
        list_e = [wrap(me_e + k + 1, n_expert) for k in range(n_expert - 1)]

    def peer_t(k):
        return list_t[k] if n_tensor <= 16 else wrap(me_t + k + 1, n_tensor)

    def peer_e(k):
        return list_e[k] if n_expert <= 16 else wrap(me_e + k + 1, n_expert)

    def over_t(src, dst, sems, index, peer):
        return pltpu.make_async_remote_copy(
            src_ref=src,
            dst_ref=dst,
            send_sem=sems.at[0, index],
            recv_sem=sems.at[1, index],
            device_id=(me_e, peer),
            device_id_type=MESH,
        )

    def over_e(src, dst, sems, index, peer):
        return pltpu.make_async_remote_copy(
            src_ref=src,
            dst_ref=dst,
            send_sem=sems.at[0, index],
            recv_sem=sems.at[1, index],
            device_id=(peer, me_t),
            device_id_type=MESH,
        )

    def await_all(sem, buffer, count, columns):
        whole = buffer.at[pl.ds(0, count), :, columns]
        pltpu.make_async_copy(whole, whole, sem).wait()

    def landed(buffer, sems, c, count):
        await_all(sems.at[1, c], buffer, count, span(c))

    def left(buffer, sems, c, count):
        await_all(sems.at[0, c], buffer, count, span(c))

    loads = [
        pltpu.make_async_copy(expert_hbm, expert_ids, in_sem.at[0]),
        pltpu.make_async_copy(slot_hbm, slot_ids, in_sem.at[1]),
        pltpu.make_async_copy(tokens_hbm, tokens, in_sem.at[2]),
        pltpu.make_async_copy(router_hbm, router, in_sem.at[3]),
        pltpu.make_async_copy(grad_hbm.at[0], hidden_grad, in_sem.at[4]),
    ]
    for load in loads[:4]:
        load.start()

    barrier = pltpu.get_barrier_semaphore()

    def greet_t(k):
        pl.semaphore_signal(
            barrier, inc=1, device_id=(me_e, peer_t(k)), device_id_type=MESH
        )

    def greet_e(k):
        pl.semaphore_signal(
            barrier, inc=1, device_id=(peer_e(k), me_t), device_id_type=MESH
        )

    each(n_tensor - 1, greet_t)
    each(n_expert - 1, greet_e)

    weight_loads = []
    for c in range(chunks):
        pair = (
            pltpu.make_async_copy(gate_hbm.at[0, span(c)], w_gate.at[span(c)], w_sem.at[0, c]),
            pltpu.make_async_copy(up_hbm.at[0, span(c)], w_up.at[span(c)], w_sem.at[1, c]),
        )
        weight_loads.append(pair)
    for load in weight_loads[0]:
        load.start()

    loads[0].wait()
    loads[1].wait()
    row_index = lax.broadcasted_iota(jnp.int32, (tok_rows, 128), 0)
    expert_of = jnp.zeros((tok_rows, 128), jnp.int32)
    slot_of = jnp.zeros((tok_rows, 128), jnp.int32)
    for i in range(tok_rows):
        expert_of = jnp.where(row_index == i, expert_ids[i], expert_of)
        slot_of = jnp.where(row_index == i, slot_ids[i], slot_of)
    ids[me_t] = expert_of * capacity + slot_of
    picked = (
        expert_of[:, :1] == lax.broadcasted_iota(jnp.int32, (tok_rows, n_expert), 1)
    ).astype(F32)

    loads[2].wait()
    loads[3].wait()
    column = jnp.dot(picked.astype(BF16), router[...], preferred_element_type=F32)
    token_values = tokens[...].astype(F32)
    score = jax.nn.sigmoid(jnp.sum(token_values * column, axis=1, keepdims=True))
    routed = (score * token_values).astype(BF16)
    rows[me_t] = routed

    pl.semaphore_wait(barrier, n_tensor + n_expert - 2)

    def send_ids(k):
        over_t(ids.at[me_t], ids.at[me_t], ids_sem, 0, peer_t(k)).start()

    each(n_tensor - 1, send_ids)
    for c in range(chunks):

        mine_rows = rows.at[me_t, :, span(c)]

        def send_rows(k):
            over_t(mine_rows, mine_rows, rows_sem, c, peer_t(k)).start()

        each(n_tensor - 1, send_rows)

    for pair in weight_loads[1:]:
        for load in pair:
            load.start()
    loads[4].start()

    await_all(ids_sem.at[1, 0], ids, n_tensor - 1, pl.ds(0, 128))
    target = ids[...].reshape(group, 128)[:, :1]
    place = (target == lax.broadcasted_iota(jnp.int32, (group, slots), 1)).astype(F32)
    place_t = place.T.astype(BF16)
    place = place.astype(BF16)

    def dispatch(c):
        landed(rows, rows_sem, c, n_tensor - 1)
        group_rows = rows[:, :, span(c)].astype(F32).reshape(group, spans[c][1]).astype(BF16)
        placed = jnp.dot(place_t, group_rows, preferred_element_type=F32)
        sent[:, :, span(c)] = placed.reshape(n_expert, capacity, spans[c][1]).astype(BF16)

        def send(k):
            peer = peer_e(k)
            over_e(sent.at[peer, :, span(c)], arrived.at[me_e, :, span(c)], slots_sem, c, peer).start()

        each(n_expert - 1, send)
        arrived[me_e, :, span(c)] = sent[me_e, :, span(c)]

    def project(c):
        landed(arrived, slots_sem, c, n_expert - 1)
        for load in weight_loads[c]:
            load.wait()
        lhs = arrived[:, :, span(c)].astype(F32).reshape(slots, spans[c][1]).astype(BF16)
        for total, weight in ((acc_gate, w_gate), (acc_up, w_up)):
            product = jnp.dot(lhs, weight[span(c)], preferred_element_type=F32)
            total[...] = product if c == 0 else total[...] + product

    for c in range(chunks):
        dispatch(c)
    for c in range(chunks):
        project(c)

    loads[4].wait()
    gate_proj = acc_gate[...]
    lifted = acc_up[...]
    cotangent = hidden_grad[...].astype(F32)
    sigma = jax.nn.sigmoid(gate_proj)
    silu = gate_proj * sigma
    slope = sigma * (1.0 + gate_proj * (1.0 - sigma))
    d_gate[...] = (cotangent * lifted * slope).astype(BF16)
    d_lifted[...] = (cotangent * silu).astype(BF16)

    contract = (((1,), (1,)), ((), ()))

    def pull_back(c):
        value = lax.dot_general(
            d_gate[...], w_gate[span(c)], contract, preferred_element_type=F32
        ) + lax.dot_general(d_lifted[...], w_up[span(c)], contract, preferred_element_type=F32)
        part[:, :, span(c)] = value.reshape(n_expert, capacity, spans[c][1]).astype(BF16)

        def send(k):
            peer = peer_e(k)
            over_e(part.at[peer, :, span(c)], returned.at[me_e, :, span(c)], part_sem, c, peer).start()

        each(n_expert - 1, send)
        returned[me_e, :, span(c)] = part[me_e, :, span(c)]

    def collect(c):
        landed(returned, part_sem, c, n_expert - 1)
        slot_rows = returned[:, :, span(c)].astype(F32).reshape(slots, spans[c][1]).astype(BF16)
        token_rows = jnp.dot(place, slot_rows, preferred_element_type=F32)
        mine[:, :, span(c)] = token_rows.reshape(n_tensor, tok_rows, spans[c][1]).astype(BF16)

        def send(k):
            peer = peer_t(k)
            over_t(mine.at[peer, :, span(c)], partials.at[me_t, :, span(c)], mine_sem, c, peer).start()

        each(n_tensor - 1, send)
        partials[me_t, :, span(c)] = mine[me_t, :, span(c)]

    def add_up(c):
        landed(partials, mine_sem, c, n_tensor - 1)
        summed = jnp.sum(partials[:, :, span(c)].astype(F32), axis=0).astype(BF16).astype(F32)
        d_rows[:, span(c)] = summed
        return jnp.sum(tokens[:, span(c)].astype(F32) * summed, axis=1, keepdims=True)

    inner = jnp.zeros((tok_rows, 1), F32)
    for c in range(chunks):
        pull_back(c)
    gate_again = acc_gate[...]
    act[0] = (gate_again * jax.nn.sigmoid(gate_again) * acc_up[...]).astype(BF16)
    for c in range(chunks):
        collect(c)
    for c in range(chunks):
        inner = inner + add_up(c)

    gradient = score * d_rows[...] + (inner * score * (1.0 - score)) * column
    out[...] = gradient.astype(BF16)

    await_all(ids_sem.at[0, 0], ids, n_tensor - 1, pl.ds(0, 128))
    for c in range(chunks):
        left(rows, rows_sem, c, n_tensor - 1)
        left(sent, slots_sem, c, n_expert - 1)
        left(part, part_sem, c, n_expert - 1)
        left(mine, mine_sem, c, n_tensor - 1)


def finish(act_in, out_in, act_out, out_out, sem):
    copies = (
        pltpu.make_async_copy(act_in, act_out, sem.at[0]),
        pltpu.make_async_copy(out_in, out_out, sem.at[1]),
    )
    for copy in copies:
        copy.start()
    for copy in copies:
        copy.wait()


def shards(tokens, expert_ids, slot_ids, router, w_gate, w_up, hidden_grad):
    n_tensor = lax.axis_size("tensor")
    n_expert = lax.axis_size("expert")
    tok_rows, width = tokens.shape
    slots, hidden = hidden_grad.shape[1:]
    capacity = slots // n_expert
    spans = cut(width)
    chunks = len(spans)
    by_expert = (n_expert, capacity, width)
    by_tensor = (n_tensor, tok_rows, width)
    dma = pltpu.SemaphoreType.DMA
    hbm = pl.BlockSpec(memory_space=pltpu.HBM)
    vmem = pl.BlockSpec(memory_space=pltpu.VMEM)
    results = pl.pallas_call(
        functools.partial(kernel, spans, n_expert, n_tensor),
        out_shape=(pltpu.VMEM(hidden_grad.shape, BF16), pltpu.VMEM(tokens.shape, BF16)),
        in_specs=[hbm] * 7,
        out_specs=(vmem, vmem),
        scratch_shapes=[
            pltpu.VMEM(tokens.shape, BF16),
            pltpu.SMEM(expert_ids.shape, jnp.int32),
            pltpu.SMEM(slot_ids.shape, jnp.int32),
            pltpu.VMEM(router.shape[::-1], BF16),
            pltpu.VMEM(w_gate.shape[1:], BF16),
            pltpu.VMEM(w_up.shape[1:], BF16),
            pltpu.VMEM((slots, hidden), BF16),
            pltpu.VMEM((n_tensor, tok_rows, 128), jnp.int32),
            pltpu.VMEM(by_tensor, BF16),
            pltpu.VMEM(by_expert, BF16),
            pltpu.VMEM(by_expert, BF16),
            pltpu.VMEM(by_expert, BF16),
            pltpu.VMEM(by_expert, BF16),
            pltpu.VMEM(by_tensor, BF16),
            pltpu.VMEM(by_tensor, BF16),
            pltpu.VMEM((slots, hidden), F32),
            pltpu.VMEM((slots, hidden), F32),
            pltpu.VMEM((slots, hidden), BF16),
            pltpu.VMEM((slots, hidden), BF16),
            pltpu.VMEM(tokens.shape, F32),
            dma((5,)),
            dma((2, chunks)),
            dma((2, 1)),
            dma((2, chunks)),
            dma((2, chunks)),
            dma((2, chunks)),
            dma((2, chunks)),
        ],
        compiler_params=pltpu.CompilerParams(
            collective_id=0, has_side_effects=True, vmem_limit_bytes=56 * 1024 * 1024
        ),
        name="routed_experts",
    )(tokens, expert_ids, slot_ids, router.T, w_gate, w_up, hidden_grad)
    results = [pltpu.with_memory_space_constraint(value, pltpu.VMEM) for value in results]
    return pl.pallas_call(
        finish,
        out_shape=(
            jax.ShapeDtypeStruct(hidden_grad.shape, BF16),
            jax.ShapeDtypeStruct(tokens.shape, BF16),
        ),
        in_specs=[vmem] * 2,
        out_specs=(hbm, hbm),
        scratch_shapes=[dma((2,))],
        name="move_results",
    )(*results)

def solution(mesh):
    in_specs = (
        P(("expert", "tensor"), None),
        P(("expert", "tensor")),
        P(("expert", "tensor")),
        P(),
        P("expert", None, "tensor"),
        P("expert", None, "tensor"),
        P("expert", None, "tensor"),
    )
    out_specs = (P("expert", None, "tensor"), P(("expert", "tensor"), None))
    return jax.shard_map(shards, mesh=mesh, in_specs=in_specs, out_specs=out_specs, check_vma=False)
```
